32 devices in a mesh: row: 8 (over z, y), snk: 4 (over x, core).
Axes of the slice: x: 2, y: 2, z: 4, core: 2. Of those that a mesh axis runs over, the one named last changes fastest.
Arguments:
- start_basis: bfloat16 [65536, 128], P(('row', 'snk')), may hold values from -6 to 6
- band_cols: int32 [65536, 3, 8], P(('row', 'snk')), may hold values from 0 to 127, as said below
- band_wts: float32 [65536, 3, 8], P(('row', 'snk')), may hold values from 0.02 to 1
- far_dst: int32 [8192], P(('row', 'snk')), may hold values from 0 to 2047
- far_src: int32 [8192], P(('row', 'snk')), may hold values from 0 to 2047
- far_wts: float32 [8192], P(('row', 'snk')), may hold values from 1 to 8
Outputs:
- embedding: float32 [65536, 128], P(('row', 'snk'))
The draws below stay inside these ranges and needn't reach their ends.
Inputs may be any that keep to these rules, and one draw needn't show every extreme that they name: `band_cols`: in each row and each of its three band blocks the 8 columns are distinct.
All inputs are finite; a program needn't handle non-finite values.
Results may differ from the reference program's by a relative error of at most 0.0047.
Values may be sent and summed in bfloat16 or wider, within the bound.
No kernel may reach another device: no remote copies, remote signals or barrier semaphores. Data moves between devices by JAX's collectives and lax.ppermute only.
A program may use at most 64 MiB of HBM per device.

```python
import math
import jax
import jax.numpy as jnp
from jax import lax

VECS = 128
BLK = 128
KB = 8
PEERS = 4
CAP = 64
DEGREE = 8
OUTER = 1
ROWS_DEV = 2048
NROWS = 65536
FAR = 8192
N_ROW = 8
N_SNK = 4


def draw_band_cols(key, part):
    key = jax.random.fold_in(key, 7)
    key_base, key_stride = jax.random.split(key)
    base_lane = jax.random.randint(key_base, (NROWS, 3, 1), 0, BLK, dtype=jnp.int32)
    stride = 2 * jax.random.randint(key_stride, (NROWS, 3, 1), 0, BLK // 2, dtype=jnp.int32) + 1
    return ((base_lane + stride * jnp.arange(KB, dtype=jnp.int32)) % BLK).astype(jnp.int32)


def place_ends(result, key, least, top_value):
    extent = result.shape
    place = [jax.random.randint(jax.random.fold_in(key, axis), (), 0, extent[axis]) for axis in range(len(extent))]
    result = result.at[tuple(place)].set(least)
    longest = extent.index(max(extent))
    place[longest] = (place[longest] + 1) % extent[longest]
    return result.at[tuple(place)].set(top_value)


def block_scale(stream_key, extent, shards, low, top_value):
    def one(dim, shards_of):
        draws = jax.random.uniform(jax.random.fold_in(jax.random.fold_in(stream_key, 6), dim), (shards_of,), jnp.float32, low / len(shards), top_value / len(shards))
        return jnp.repeat(jnp.exp(draws), extent[dim] // shards_of).reshape((-1,) + (1,) * (len(extent) - dim - 1))

    gain = one(*shards[0])
    for cut in shards[1:]:
        gain = gain * one(*cut)
    return gain


def normal_values(own_key, dims, scale, bound, cuts=(), held_as=jnp.bfloat16):
    level = block_scale(own_key, dims, cuts, -0.22, 0.18) if cuts else 1.0
    values = jax.random.normal(own_key, dims, jnp.float32) * scale * level
    return jnp.minimum(jnp.maximum(values, -bound), bound).astype(held_as)


def setup_inputs(seed: int = 0) -> dict:
    arg_keys = jax.random.split(jax.random.key(seed), 7)
    start_basis = normal_values(arg_keys[0], (NROWS, VECS), 1.0, 6.0, ((0, 32),))
    band_cols = draw_band_cols(jax.random.fold_in(arg_keys[6], 71), 0)
    band_wts = jnp.clip(jnp.exp(math.log(1.0) - 3.912023 * jax.random.uniform(arg_keys[2], (NROWS, 3, KB), jnp.float32) ** block_scale(arg_keys[2], (NROWS, 3, KB), ((0, 32),), -0.2, 0.2)), 0.02, 1.0)
    far_dst = place_ends(jax.random.randint(arg_keys[3], (FAR,), 0, ROWS_DEV), jax.random.fold_in(arg_keys[3], 1), 0, ROWS_DEV - 1).astype(jnp.int32)
    far_src = place_ends(jax.random.randint(arg_keys[4], (FAR,), 0, ROWS_DEV), jax.random.fold_in(arg_keys[4], 1), 0, ROWS_DEV - 1).astype(jnp.int32)
    far_wts = jnp.clip(jnp.exp(math.log(8.0) - 2.0794415 * jax.random.uniform(arg_keys[5], (FAR,), jnp.float32) ** block_scale(arg_keys[5], (FAR,), ((0, 32),), -0.2, 0.2)), 1.0, 8.0)
    return {"start_basis": start_basis, "band_cols": band_cols, "band_wts": band_wts, "far_dst": far_dst, "far_src": far_src, "far_wts": far_wts}


HALF_WIDTH = 0.95

def reference(start_basis, band_cols, band_wts, far_dst, far_src, far_wts):
    devices = N_ROW * N_SNK
    total_rows = start_basis.shape[0]
    block_count = total_rows // BLK
    row_ids = jnp.arange(total_rows, dtype=jnp.int32)
    edge_ids = jnp.arange(far_dst.shape[0], dtype=jnp.int32)
    owners = edge_ids // (CAP * PEERS)
    groups = edge_ids % (CAP * PEERS) // CAP
    distance = 2 ** (groups // 2 + 1) * (1 - 2 * (groups % 2))
    peers = (owners + distance + devices) % devices
    far_from = (owners * ROWS_DEV + far_dst).astype(jnp.int32)
    far_to = (peers * ROWS_DEV + far_src).astype(jnp.int32)
    degree = lax.optimization_barrier(jnp.sum(band_wts, axis=(1, 2))) + jax.ops.segment_sum(far_wts, far_from, num_segments=total_rows)
    band_coef = (band_wts / degree[:, None, None]).astype(jnp.bfloat16)
    far_coef = far_wts / degree[far_from]
    offsets = jnp.arange(3, dtype=jnp.int32) - 1
    block_ids = row_ids // BLK
    target = (block_ids[:, None] + offsets[None, :]) % block_count * BLK
    columns = (target[:, :, None] + band_cols).reshape(total_rows, 3 * KB).astype(jnp.int32)
    coef_flat = band_coef.reshape(total_rows, 3 * KB)
    slab_rows = ROWS_DEV

    def walk(values):
        packed = values.astype(jnp.bfloat16)

        def gather_slab(slab_pair):
            slab_cols, slab_coef = slab_pair
            picked = packed[slab_cols].astype(jnp.float32)
            return jnp.einsum('rk,rkv->rv', slab_coef.astype(jnp.float32), picked, precision=lax.Precision.HIGHEST)
        band_term = lax.map(gather_slab, (columns.reshape(-1, slab_rows, 3 * KB), coef_flat.reshape(-1, slab_rows, 3 * KB)))
        band_term = band_term.reshape(total_rows, VECS)
        far_term = jax.ops.segment_sum(far_coef[:, None] * packed[far_to].astype(jnp.float32), far_from, num_segments=total_rows)
        return band_term + far_term
    basis_now = start_basis.astype(jnp.float32)
    for outer_step in range(OUTER):
        previous = basis_now
        current = walk(basis_now) / HALF_WIDTH
        for degree_step in range(DEGREE - 1):
            following = 2.0 / HALF_WIDTH * walk(current) - previous
            previous, current = (current, following)
        gram_total = jnp.dot(current.T.astype(jnp.float32), current.astype(jnp.float32), precision=lax.Precision.HIGHEST, preferred_element_type=jnp.float32)
        factor = jnp.linalg.cholesky(gram_total)
        basis_now = jax.scipy.linalg.solve_triangular(factor, current.T, lower=True).T
    return basis_now * math.sqrt(total_rows)
```

```python
import math

import jax
import jax.numpy as jnp
from jax import lax
from jax.experimental import pallas as pl
from jax.experimental.pallas import tpu as pltpu
from jax.sharding import PartitionSpec as P

VECS = 128
BLK = 128
KB = 8
PEERS = 4
CAP = 64
DEGREE = 8
HALF_WIDTH = 0.95
AXES = ("row", "snk")
FAR = (2, 4)
BF16 = jnp.bfloat16
F32 = jnp.float32
VMEM = pl.BlockSpec(memory_space=pltpu.VMEM)
SMEM = pl.BlockSpec(memory_space=pltpu.SMEM)
PARAMS = pltpu.CompilerParams(vmem_limit_bytes=24 * 1024 * 1024)


def swap_pairs(count, by, odd):
    pairs = []
    for low in range(count):
        if (low // by) % 2 == odd:
            high = (low + by) % count
            pairs += [(low, high), (high, low)]
    return pairs


def split3(value):
    high = value.astype(BF16)
    rest = value - high.astype(F32)
    mid = rest.astype(BF16)
    low = (rest - mid.astype(F32)).astype(BF16)
    return high, mid, low


def stacked(value, height):
    parts = split3(value)
    pad = jnp.zeros((height - 3, value.shape[1]), BF16)
    return jnp.concatenate([*parts, pad], axis=0)


def dot(a, b, dims, precision=None):
    return lax.dot_general(
        a, b, (dims, ((), ())), precision=precision, preferred_element_type=F32
    )


def prepare_kernel(cols_ref, wts_ref, dst_ref, far_ref, band_ref, far_mat_ref):
    rows = cols_ref.shape[2]
    edges = dst_ref.shape[1]
    dst = dst_ref[...]
    far = far_ref[...]
    for b in range(rows // BLK):
        ids = lax.broadcasted_iota(jnp.int32, (BLK, edges), 0) + b * BLK
        far_mat_ref[pl.ds(b * BLK, BLK), :] = jnp.where(ids == dst, 1.0, 0.0).astype(BF16)
    hot = far_mat_ref[...]
    far_sum = jnp.sum(dot(stacked(far, 16), hot, ((1,), (1,))), axis=0, keepdims=True)
    degree = far_sum
    for o in range(3):
        degree = degree + jnp.sum(wts_ref[o], axis=0, keepdims=True)
    at_edge = jnp.sum(dot(stacked(degree, 16), hot, ((1,), (0,))), axis=0, keepdims=True)
    far_coef = (far / at_edge).astype(BF16)
    for b in range(rows // BLK):
        block = pl.ds(b * BLK, BLK)
        far_mat_ref[block, :] = far_mat_ref[block, :] * far_coef
        degree_b = degree[:, b * BLK : (b + 1) * BLK]
        for o in range(3):
            cols = cols_ref[o, :, block]
            coef = (wts_ref[o, :, block] / degree_b).astype(BF16).astype(F32)
            ids = lax.broadcasted_iota(jnp.int32, (BLK, BLK), 0)
            dense = jnp.zeros((BLK, BLK), F32)
            for k in range(KB):
                dense = jnp.where(ids == cols[k : k + 1, :], coef[k : k + 1, :], dense)
            band_ref[block, pl.ds(o * BLK, BLK)] = dense.T.astype(BF16)


def prepare(cols, wts, dst, far):
    rows, edges = cols.shape[2], dst.shape[1]
    return pl.pallas_call(
        prepare_kernel,
        out_shape=(
            jax.ShapeDtypeStruct((rows, 3 * BLK), BF16),
            jax.ShapeDtypeStruct((rows, edges), BF16),
        ),
        in_specs=[VMEM] * 4,
        out_specs=(VMEM, VMEM),
        compiler_params=PARAMS,
        name="prepare",
    )(cols, wts, dst, far)


def send_out(even, first, last, picked, edge_refs, pick_refs):
    edge_refs[0][...] = jnp.where(even, last, first)
    edge_refs[1][...] = jnp.where(even, first, last)
    for g in range(PEERS):
        pick_refs[g][...] = picked[g * CAP : (g + 1) * CAP].astype(BF16)


def first_kernel(even_ref, field_ref, w0, w1, w2, w3, pick_mat_ref, e0, e1, p0, p1, p2, p3):
    rows = field_ref.shape[0]
    half = 2 * CAP
    for g, (a, b) in enumerate(((w0, w1), (w2, w3))):
        wanted = jnp.concatenate([a[...], b[...]], axis=1)
        column = jnp.broadcast_to(wanted.astype(F32), (half, half)).T
        for b in range(rows // BLK):
            ids = lax.broadcasted_iota(jnp.int32, (half, BLK), 1) + b * BLK
            hot = jnp.where(column == ids.astype(F32), 1.0, 0.0).astype(BF16)
            pick_mat_ref[pl.ds(g * half, half), pl.ds(b * BLK, BLK)] = hot
    field = field_ref[...]
    picked = dot(pick_mat_ref[...], field, ((1,), (0,)))
    send_out(even_ref[0] == 0, field[:BLK], field[rows - BLK :], picked, (e0, e1), (p0, p1, p2, p3))


SENT = (
    *(jax.ShapeDtypeStruct((BLK, VECS), BF16),) * 2,
    *(jax.ShapeDtypeStruct((CAP, VECS), BF16),) * PEERS,
)


def first(even, field, wanted):
    rows = field.shape[0]
    return pl.pallas_call(
        first_kernel,
        out_shape=(jax.ShapeDtypeStruct((PEERS * CAP, rows), BF16), *SENT),
        in_specs=[SMEM] + [VMEM] * 5,
        out_specs=(VMEM,) * 7,
        compiler_params=PARAMS,
        name="first",
    )(even, field, *wanted)


def advance(even_ref, band_ref, far_mat_ref, field_ref, prev_ref, got, scale, store):
    rows = field_ref.shape[0]
    count = rows // BLK
    even = even_ref[0] == 0
    low = jnp.where(even, got[1][...], got[0][...])
    high = jnp.where(even, got[0][...], got[1][...])
    far = jnp.concatenate([g[...] for g in got[2:]], axis=0)
    for b in range(count):
        block = pl.ds(b * BLK, BLK)
        total = dot(far_mat_ref[block, :], far, ((1,), (0,)))
        if b == 0:
            total += dot(band_ref[block, :BLK], low, ((1,), (0,)))
            total += dot(band_ref[block, BLK:], field_ref[: 2 * BLK, :], ((1,), (0,)))
        elif b == count - 1:
            total += dot(
                band_ref[block, : 2 * BLK], field_ref[rows - 2 * BLK :, :], ((1,), (0,))
            )
            total += dot(band_ref[block, 2 * BLK :], high, ((1,), (0,)))
        else:
            total += dot(
                band_ref[block, :], field_ref[pl.ds((b - 1) * BLK, 3 * BLK), :], ((1,), (0,))
            )
        value = total * scale
        if prev_ref is not None:
            value = value - prev_ref[block, :].astype(F32)
        store(block, value)
    return even


def step_kernel(scale, has_prev, *refs):
    even_ref, band_ref, far_mat_ref, pick_mat_ref, field_ref = refs[:5]
    refs = refs[5:]
    prev_ref = None
    if has_prev:
        prev_ref, refs = refs[0], refs[1:]
    got, refs = refs[:6], refs[6:]
    next_ref, packed_ref, sent = refs[0], refs[1], refs[2:]

    def store(block, value):
        next_ref[block, :] = value
        packed_ref[block, :] = value.astype(BF16)

    even = advance(even_ref, band_ref, far_mat_ref, field_ref, prev_ref, got, scale, store)
    rows = field_ref.shape[0]
    picked = dot(pick_mat_ref[...], packed_ref[...], ((1,), (0,)))
    send_out(
        even, packed_ref[:BLK, :], packed_ref[rows - BLK :, :], picked, sent[:2], sent[2:]
    )


def step(scale, even, mats, field, prev, got):
    rows = field.shape[0]
    has_prev = prev is not None
    before = (prev,) if has_prev else ()
    return pl.pallas_call(
        lambda *refs: step_kernel(scale, has_prev, *refs),
        out_shape=(
            jax.ShapeDtypeStruct((rows, VECS), F32),
            jax.ShapeDtypeStruct((rows, VECS), BF16),
            *SENT,
        ),
        in_specs=[SMEM] + [VMEM] * (10 + len(before)),
        out_specs=(VMEM,) * 8,
        compiler_params=PARAMS,
        name="step",
    )(even, *mats, field, *before, *got)


def last_kernel(scale, *refs):
    even_ref, band_ref, far_mat_ref, field_ref, prev_ref = refs[:5]
    got, (next_ref, gram_ref) = refs[5:11], refs[11:]

    def store(block, value):
        next_ref[block, :] = value

    advance(even_ref, band_ref, far_mat_ref, field_ref, prev_ref, got, scale, store)
    value = next_ref[...]
    gram_ref[...] = dot(value, value, ((0,), (0,)), lax.Precision.HIGHEST)


def last(scale, even, band, far_mat, field, prev, got):
    rows = field.shape[0]
    return pl.pallas_call(
        lambda *refs: last_kernel(scale, *refs),
        out_shape=(
            jax.ShapeDtypeStruct((rows, VECS), F32),
            jax.ShapeDtypeStruct((VECS, VECS), F32),
        ),
        in_specs=[SMEM] + [VMEM] * 10,
        out_specs=(VMEM, VMEM),
        compiler_params=PARAMS,
        name="last",
    )(even, band, far_mat, field, prev, *got)


def summed(value, count):
    bits = [1 << i for i in range(count.bit_length() - 1)]
    stages = [bits[:1]] + [bits[i : i + 2] for i in range(1, len(bits), 2)]
    for stage in stages:
        masks = [stage[0]] if len(stage) == 1 else [*stage, stage[0] ^ stage[1]]
        total = value
        for mask in masks:
            total = total + lax.ppermute(value, AXES, [(i, i ^ mask) for i in range(count)])
        value = total
    return value


def local(start_basis, band_cols, band_wts, far_dst, far_src, far_wts):
    count = lax.axis_size(AXES)
    place = lax.axis_index(AXES)
    total_rows = start_basis.shape[0] * count

    def swap(value, by, odd):
        return lax.ppermute(value, AXES, swap_pairs(count, by, odd))

    def by_swap(edges):
        groups = edges.reshape(PEERS, CAP)
        ordered = []
        for i, by in enumerate(FAR):
            even = (place // by) % 2 == 0
            ahead, back = groups[2 * i : 2 * i + 1], groups[2 * i + 1 : 2 * i + 2]
            ordered += [jnp.where(even, ahead, back), jnp.where(even, back, ahead)]
        return ordered

    swaps = [(by, odd) for by in FAR for odd in (0, 1)]
    wanted = [swap(g, *s) for g, s in zip(by_swap(far_src), swaps)]
    dst = jnp.concatenate(by_swap(far_dst), axis=1)
    far = jnp.concatenate(by_swap(far_wts), axis=1)
    band, far_mat = prepare(
        jnp.transpose(band_cols, (1, 2, 0)), jnp.transpose(band_wts, (1, 2, 0)), dst, far
    )
    even = (place % 2).astype(jnp.int32).reshape(1)
    pick_mat, *sent = first(even, start_basis, wanted)

    def exchange(sent):
        return [swap(v, *s) for v, s in zip(sent, [(1, 0), (1, 1), *swaps])]

    mats = (band, far_mat, pick_mat)
    got = exchange(sent)
    previous, packed = start_basis, start_basis
    current, packed, *sent = step(1.0 / HALF_WIDTH, even, mats, packed, None, got)
    for _ in range(DEGREE - 2):
        got = exchange(sent)
        following, packed, *sent = step(2.0 / HALF_WIDTH, even, mats, packed, previous, got)
        previous, current = current, following
    got = exchange(sent)
    filtered, gram = last(2.0 / HALF_WIDTH, even, band, far_mat, packed, previous, got)
    factor = jnp.linalg.cholesky(summed(gram, count))
    basis = jax.scipy.linalg.solve_triangular(factor, filtered.T, lower=True).T
    return basis * math.sqrt(total_rows)


def solution(mesh):
    placed = (
        P(AXES, None),
        P(AXES, None, None),
        P(AXES, None, None),
        P(AXES),
        P(AXES),
        P(AXES),
    )
    return jax.shard_map(
        local, mesh=mesh, in_specs=placed, out_specs=P(AXES, None), check_vma=False
    )
```

```python
import math

import jax
import jax.numpy as jnp
from jax import lax
from jax.experimental import pallas as pl
from jax.experimental.pallas import tpu as pltpu
from jax.sharding import PartitionSpec as P

VECS = 128
BLK = 128
KB = 8
PEERS = 4
CAP = 64
DEGREE = 8
HALF_WIDTH = 0.95
AXES = ("row", "snk")
FAR = (2, 4)
LINKS = ((4, 1), (2, 1), (1, 1), (4, 0), (2, 0), (1, 0))
FAR_LINKS = tuple((by, odd) for by in FAR for odd in (0, 1))
BF16 = jnp.bfloat16
F32 = jnp.float32
VMEM = pl.BlockSpec(memory_space=pltpu.VMEM)
ANY = pl.BlockSpec(memory_space=pl.ANY)
SMEM = pl.BlockSpec(memory_space=pltpu.SMEM)
PARAMS = pltpu.CompilerParams(vmem_limit_bytes=24 * 1024 * 1024)


def swap_pairs(count, by, odd):
    pairs = []
    for low in range(count):
        if (low // by) % 2 == odd:
            high = (low + by) % count
            pairs += [(low, high), (high, low)]
    return pairs


def split3(value):
    high = value.astype(BF16)
    rest = value - high.astype(F32)
    mid = rest.astype(BF16)
    low = (rest - mid.astype(F32)).astype(BF16)
    return high, mid, low


def stacked(value, height):
    parts = split3(value)
    pad = jnp.zeros((height - 3, value.shape[1]), BF16)
    return jnp.concatenate([*parts, pad], axis=0)


def dot(a, b, dims, precision=None):
    return lax.dot_general(
        a, b, (dims, ((), ())), precision=precision, preferred_element_type=F32
    )


def is_low(place_ref, by):
    return lax.rem(lax.div(place_ref[0], by), 2) == 0


def turned(row):
    half = row.shape[1] // 2
    return jnp.concatenate([row[:, half:], row[:, :half]], axis=1)


def by_link(place_ref, row):
    parts = []
    for i, by in enumerate(FAR):
        pair = row[:, 2 * CAP * i : 2 * CAP * (i + 1)]
        parts.append(jnp.where(is_low(place_ref, by), pair, turned(pair)))
    return jnp.concatenate(parts, axis=1)


def as_columns(row):
    return jnp.broadcast_to(row, (row.shape[1], row.shape[1])).T


def prepare_kernel(
    place_ref, cols_any, wts_any, dst_ref, far_ref, band_ref, hot_ref, coef_ref, cols_ref, wts_ref, sems
):
    copies = [
        pltpu.make_async_copy(cols_any, cols_ref, sems.at[0]),
        pltpu.make_async_copy(wts_any, wts_ref, sems.at[1]),
    ]
    for copy in copies:
        copy.start()
    rows = cols_ref.shape[2]
    edges = dst_ref.shape[1]
    dst = by_link(place_ref, dst_ref[...])
    far = by_link(place_ref, far_ref[...])
    for b in range(rows // BLK):
        ids = lax.broadcasted_iota(jnp.int32, (BLK, edges), 0) + b * BLK
        hot_ref[pl.ds(b * BLK, BLK), :] = jnp.where(ids == dst, 1.0, 0.0).astype(BF16)
    hot = hot_ref[...]
    degree = jnp.sum(dot(stacked(far, 16), hot, ((1,), (1,))), axis=0, keepdims=True)
    for copy in copies:
        copy.wait()
    for o in range(3):
        degree = degree + jnp.sum(wts_ref[o], axis=0, keepdims=True)
    at_edge = jnp.sum(dot(stacked(degree, 16), hot, ((1,), (0,))), axis=0, keepdims=True)
    far_coef = far / at_edge
    for i in range(edges // BLK):
        coef_ref[pl.ds(i * BLK, BLK), :] = as_columns(far_coef[:, i * BLK : (i + 1) * BLK])
    ids = lax.broadcasted_iota(jnp.int32, (BLK, BLK), 0)
    for b in range(rows // BLK):
        block = pl.ds(b * BLK, BLK)
        degree_b = degree[:, b * BLK : (b + 1) * BLK]
        for o in range(3):
            cols = cols_ref[o, :, block]
            coef = (wts_ref[o, :, block] / degree_b).astype(BF16).astype(F32)
            dense = jnp.zeros((BLK, BLK), F32)
            for k in range(KB):
                dense = jnp.where(ids == cols[k : k + 1, :], coef[k : k + 1, :], dense)
            band_ref[block, pl.ds(o * BLK, BLK)] = dense.T.astype(BF16)


def prepare(place, cols, wts, dst, far):
    rows, edges = cols.shape[2], dst.shape[1]
    return pl.pallas_call(
        prepare_kernel,
        out_shape=(
            jax.ShapeDtypeStruct((rows, 3 * BLK), BF16),
            jax.ShapeDtypeStruct((rows, edges), BF16),
            jax.ShapeDtypeStruct((edges, VECS), F32),
        ),
        in_specs=[SMEM, ANY, ANY, VMEM, VMEM],
        out_specs=(VMEM,) * 3,
        scratch_shapes=[
            pltpu.VMEM(cols.shape, jnp.int32),
            pltpu.VMEM(wts.shape, F32),
            pltpu.SemaphoreType.DMA((2,)),
        ],
        compiler_params=PARAMS,
        name="prepare",
    )(place, cols, wts, dst, far)


def send_out(even, first, last, picked, sent):
    sent = dict(zip(LINKS, sent, strict=True))
    sent[1, 0][...] = jnp.where(even, last, first)
    sent[1, 1][...] = jnp.where(even, first, last)
    for g, link in enumerate(FAR_LINKS):
        sent[link][:CAP, :] = picked[g * CAP : (g + 1) * CAP].astype(BF16)


def first_kernel(place_ref, field_ref, w0, w1, w2, w3, pick_mat_ref, *sent):
    rows = field_ref.shape[0]
    half = 2 * CAP
    lanes = lax.broadcasted_iota(jnp.int32, (1, half), 1)
    for i, (by, pair) in enumerate(zip(FAR, ((w0, w1), (w2, w3)), strict=True)):
        ahead, back = (w[:, i * half : (i + 1) * half] for w in pair)
        low = is_low(place_ref, by)
        ahead = jnp.where(low, turned(ahead), ahead)
        back = jnp.where(low, turned(back), back)
        wanted = jnp.where(lanes < CAP, ahead, back)
        column = as_columns(wanted.astype(F32))
        for b in range(rows // BLK):
            ids = lax.broadcasted_iota(jnp.int32, (half, BLK), 1) + b * BLK
            hot = jnp.where(column == ids.astype(F32), 1.0, 0.0).astype(BF16)
            pick_mat_ref[pl.ds(i * half, half), pl.ds(b * BLK, BLK)] = hot
    field = field_ref[...]
    picked = dot(pick_mat_ref[...], field, ((1,), (0,)))
    send_out(is_low(place_ref, 1), field[:BLK], field[rows - BLK :], picked, sent)


SENT = tuple(jax.ShapeDtypeStruct((BLK, VECS), BF16) for _ in LINKS)


def first(place, field, wanted):
    rows = field.shape[0]
    return pl.pallas_call(
        first_kernel,
        out_shape=(jax.ShapeDtypeStruct((PEERS * CAP, rows), BF16), *SENT),
        in_specs=[SMEM] + [VMEM] * 5,
        out_specs=(VMEM,) * 7,
        compiler_params=PARAMS,
        name="first",
    )(place, field, *wanted)


def advance(place_ref, band_ref, hot_ref, coef_ref, field_ref, prev_ref, got, scale, store):
    rows = field_ref.shape[0]
    count = rows // BLK
    even = is_low(place_ref, 1)
    got = dict(zip(LINKS, got, strict=True))
    low = jnp.where(even, got[1, 1][...], got[1, 0][...])
    high = jnp.where(even, got[1, 0][...], got[1, 1][...])
    far = jnp.concatenate([got[link][:CAP, :] for link in FAR_LINKS], axis=0)
    far = far.astype(F32) * coef_ref[...]
    far_high = far.astype(BF16)
    far_low = (far - far_high.astype(F32)).astype(BF16)
    for b in range(count):
        block = pl.ds(b * BLK, BLK)
        total = dot(hot_ref[block, :], far_high, ((1,), (0,)))
        total += dot(hot_ref[block, :], far_low, ((1,), (0,)))
        if b == 0:
            total += dot(band_ref[block, :BLK], low, ((1,), (0,)))
            total += dot(band_ref[block, BLK:], field_ref[: 2 * BLK, :], ((1,), (0,)))
        elif b == count - 1:
            total += dot(
                band_ref[block, : 2 * BLK], field_ref[rows - 2 * BLK :, :], ((1,), (0,))
            )
            total += dot(band_ref[block, 2 * BLK :], high, ((1,), (0,)))
        else:
            total += dot(
                band_ref[block, :], field_ref[pl.ds((b - 1) * BLK, 3 * BLK), :], ((1,), (0,))
            )
        value = total * scale
        if prev_ref is not None:
            value = value - prev_ref[block, :].astype(F32)
        store(block, value)
    return even


def step_kernel(scale, has_prev, *refs):
    place_ref, band_ref, hot_ref, coef_ref, pick_mat_ref, field_ref = refs[:6]
    refs = refs[6:]
    prev_ref = None
    if has_prev:
        prev_ref, refs = refs[0], refs[1:]
    got, refs = refs[:6], refs[6:]
    next_ref, packed_ref, sent = refs[0], refs[1], refs[2:]

    def store(block, value):
        next_ref[block, :] = value
        packed_ref[block, :] = value.astype(BF16)

    even = advance(
        place_ref, band_ref, hot_ref, coef_ref, field_ref, prev_ref, got, scale, store
    )
    rows = field_ref.shape[0]
    picked = dot(pick_mat_ref[...], packed_ref[...], ((1,), (0,)))
    send_out(even, packed_ref[:BLK, :], packed_ref[rows - BLK :, :], picked, sent)


def step(scale, place, mats, field, prev, got):
    rows = field.shape[0]
    has_prev = prev is not None
    before = (prev,) if has_prev else ()
    return pl.pallas_call(
        lambda *refs: step_kernel(scale, has_prev, *refs),
        out_shape=(
            jax.ShapeDtypeStruct((rows, VECS), F32),
            jax.ShapeDtypeStruct((rows, VECS), BF16),
            *SENT,
        ),
        in_specs=[SMEM] + [VMEM] * (11 + len(before)),
        out_specs=(VMEM,) * 8,
        compiler_params=PARAMS,
        name="step",
    )(place, *mats, field, *before, *got)


def last_kernel(scale, *refs):
    place_ref, band_ref, hot_ref, coef_ref, field_ref, prev_ref = refs[:6]
    got, (next_ref, gram_ref) = refs[6:12], refs[12:]

    def store(block, value):
        next_ref[block, :] = value

    advance(
        place_ref, band_ref, hot_ref, coef_ref, field_ref, prev_ref, got, scale, store
    )
    value = next_ref[...]
    gram_ref[...] = dot(value, value, ((0,), (0,)), lax.Precision.HIGHEST)


def last(scale, place, mats, field, prev, got):
    rows = field.shape[0]
    return pl.pallas_call(
        lambda *refs: last_kernel(scale, *refs),
        out_shape=(
            jax.ShapeDtypeStruct((rows, VECS), F32),
            jax.ShapeDtypeStruct((VECS, VECS), F32),
        ),
        in_specs=[SMEM] + [VMEM] * 11,
        out_specs=(VMEM, VMEM),
        compiler_params=PARAMS,
        name="last",
    )(place, *mats, field, prev, *got)


def finish_kernel(scale, gram_ref, field_ref, out_ref, inverse_ref):
    height = 8
    count = VECS // height
    ids = lax.broadcasted_iota(jnp.int32, (height, VECS), 0)
    lanes = lax.broadcasted_iota(jnp.int32, (height, VECS), 1)
    left = [gram_ref[height * b : height * (b + 1), :] for b in range(count)]
    right = [jnp.where(ids + height * b == lanes, 1.0, 0.0) for b in range(count)]
    for j in range(VECS):
        own, at = divmod(j, height)
        row, row_right = left[own][at : at + 1, :], right[own][at : at + 1, :]
        pivot = row[:, j : j + 1]
        inverse_ref[j : j + 1, :] = row_right * (lax.rsqrt(pivot) * scale)
        by_pivot = 1.0 / pivot
        row, row_right = row * by_pivot, row_right * by_pivot
        for b in range(own + (at == height - 1), count):
            factor = left[b][:, j : j + 1]
            if b == own:
                factor = jnp.where(ids[:, :1] > at, factor, 0.0)
            left[b] = left[b] - factor * row
            right[b] = right[b] - factor * row_right
    out_ref[...] = dot(field_ref[...], inverse_ref[...], ((1,), (1,)), lax.Precision.HIGHEST)


def finish(scale, gram, field):
    return pl.pallas_call(
        lambda *refs: finish_kernel(scale, *refs),
        out_shape=jax.ShapeDtypeStruct(field.shape, F32),
        in_specs=[VMEM] * 2,
        out_specs=VMEM,
        scratch_shapes=[pltpu.VMEM((VECS, VECS), F32)],
        compiler_params=PARAMS,
        name="finish",
    )(gram, field)


def summed(value, count):
    bits = [1 << i for i in range(count.bit_length() - 1)]
    stages = [bits[:1]] + [bits[i : i + 2] for i in range(1, len(bits), 2)]
    for stage in stages:
        masks = [stage[0]] if len(stage) == 1 else [*stage, stage[0] ^ stage[1]]
        total = value
        for mask in masks:
            total = total + lax.ppermute(value, AXES, [(i, i ^ mask) for i in range(count)])
        value = total
    return value


def local(start_basis, band_cols, band_wts, far_dst, far_src, far_wts):
    count = lax.axis_size(AXES)
    place = lax.axis_index(AXES)
    total_rows = start_basis.shape[0] * count

    def swap(value, by, odd):
        return lax.ppermute(value, AXES, swap_pairs(count, by, odd))

    def as_row(value):
        return value.reshape(1, -1)

    asked = as_row(far_src)
    wanted = [swap(asked, *link) for link in FAR_LINKS]
    here = place.astype(jnp.int32).reshape(1)
    band, hot, coef = prepare(
        here,
        jnp.transpose(band_cols, (1, 2, 0)),
        jnp.transpose(band_wts, (1, 2, 0)),
        as_row(far_dst),
        as_row(far_wts),
    )
    wanted, band = lax.optimization_barrier((wanted, band))
    pick_mat, *sent = first(here, start_basis, wanted)

    def exchange(sent):
        return [swap(v, *link) for v, link in zip(sent, LINKS, strict=True)]

    previous, packed = start_basis, start_basis
    mats = (band, hot, coef, pick_mat)
    got = exchange(sent)
    current, packed, *sent = step(1.0 / HALF_WIDTH, here, mats, packed, None, got)
    for _ in range(DEGREE - 2):
        got = exchange(sent)
        following, packed, *sent = step(2.0 / HALF_WIDTH, here, mats, packed, previous, got)
        previous, current = current, following
    got = exchange(sent)
    filtered, gram = last(2.0 / HALF_WIDTH, here, mats[:3], packed, previous, got)
    return finish(math.sqrt(total_rows), summed(gram, count), filtered)


def solution(mesh):
    placed = (
        P(AXES, None),
        P(AXES, None, None),
        P(AXES, None, None),
        P(AXES),
        P(AXES),
        P(AXES),
    )
    return jax.shard_map(
        local, mesh=mesh, in_specs=placed, out_specs=P(AXES, None), check_vma=False
    )
```

```python
import math

import jax
import jax.numpy as jnp
from jax import lax
from jax.experimental import pallas as pl
from jax.experimental.pallas import tpu as pltpu
from jax.sharding import PartitionSpec as P

VECS = 128
BLK = 128
KB = 8
PEERS = 4
CAP = 64
DEGREE = 8
HALF_WIDTH = 0.95
AXES = ("row", "snk")
FAR = (2, 4)
LINKS = ((4, 1), (2, 1), (1, 1), (4, 0), (2, 0), (1, 0))
FAR_LINKS = tuple((by, odd) for by in FAR for odd in (0, 1))
BF16 = jnp.bfloat16
F32 = jnp.float32
VMEM = pl.BlockSpec(memory_space=pltpu.VMEM)
HBM = pl.BlockSpec(memory_space=pltpu.HBM)
SMEM = pl.BlockSpec(memory_space=pltpu.SMEM)
PARAMS = pltpu.CompilerParams(vmem_limit_bytes=24 * 1024 * 1024)


def swap_pairs(count, by, odd):
    pairs = []
    for low in range(count):
        if (low // by) % 2 == odd:
            high = (low + by) % count
            pairs += [(low, high), (high, low)]
    return pairs


def split3(value):
    high = value.astype(BF16)
    rest = value - high.astype(F32)
    mid = rest.astype(BF16)
    low = (rest - mid.astype(F32)).astype(BF16)
    return high, mid, low


def stacked(value, height):
    parts = split3(value)
    pad = jnp.zeros((height - 3, value.shape[1]), BF16)
    return jnp.concatenate([*parts, pad], axis=0)


def dot(a, b, dims, precision=None):
    return lax.dot_general(
        a, b, (dims, ((), ())), precision=precision, preferred_element_type=F32
    )


def is_low(place_ref, by):
    return lax.rem(lax.div(place_ref[0], by), 2) == 0


def turned(row):
    half = row.shape[1] // 2
    return jnp.concatenate([row[:, half:], row[:, :half]], axis=1)


def by_link(place_ref, row):
    parts = []
    for i, by in enumerate(FAR):
        pair = row[:, 2 * CAP * i : 2 * CAP * (i + 1)]
        parts.append(jnp.where(is_low(place_ref, by), pair, turned(pair)))
    return jnp.concatenate(parts, axis=1)


def as_columns(row):
    return jnp.broadcast_to(row, (row.shape[1], row.shape[1])).T


def prepare_kernel(
    place_ref,
    dst_any,
    far_any,
    wts_any,
    cols_any,
    field_any,
    band_ref,
    hot_ref,
    coef_ref,
    field_ref,
    dst_ref,
    far_ref,
    wts_ref,
    cols_ref,
    sems,
):
    copies = [
        pltpu.make_async_copy(source, target, sems.at[i])
        for i, (source, target) in enumerate(
            (
                (dst_any, dst_ref),
                (far_any, far_ref),
                (wts_any, wts_ref),
                (cols_any, cols_ref),
                (field_any, field_ref),
            )
        )
    ]
    for copy in copies:
        copy.start()
    copies[0].wait()
    copies[1].wait()
    rows = cols_ref.shape[2]
    edges = dst_ref.shape[1]
    dst = by_link(place_ref, dst_ref[...])
    far = by_link(place_ref, far_ref[...])
    for b in range(rows // BLK):
        ids = lax.broadcasted_iota(jnp.int32, (BLK, edges), 0) + b * BLK
        hot_ref[pl.ds(b * BLK, BLK), :] = jnp.where(ids == dst, 1.0, 0.0).astype(BF16)
    hot = hot_ref[...]
    degree = jnp.sum(dot(stacked(far, 16), hot, ((1,), (1,))), axis=0, keepdims=True)
    copies[2].wait()
    for o in range(3):
        degree = degree + jnp.sum(wts_ref[o], axis=0, keepdims=True)
    at_edge = jnp.sum(dot(stacked(degree, 16), hot, ((1,), (0,))), axis=0, keepdims=True)
    far_coef = far / at_edge
    for i in range(edges // BLK):
        coef_ref[pl.ds(i * BLK, BLK), :] = as_columns(far_coef[:, i * BLK : (i + 1) * BLK])
    copies[3].wait()
    ids = lax.broadcasted_iota(jnp.int32, (BLK, BLK), 0)
    for b in range(rows // BLK):
        block = pl.ds(b * BLK, BLK)
        degree_b = degree[:, b * BLK : (b + 1) * BLK]
        for o in range(3):
            cols = cols_ref[o, :, block]
            coef = (wts_ref[o, :, block] / degree_b).astype(BF16).astype(F32)
            dense = jnp.zeros((BLK, BLK), F32)
            for k in range(KB):
                dense = jnp.where(ids == cols[k : k + 1, :], coef[k : k + 1, :], dense)
            band_ref[block, pl.ds(o * BLK, BLK)] = dense.T.astype(BF16)
    copies[4].wait()


def prepare(place, dst, far, wts, cols, field):
    rows, edges = cols.shape[2], dst.shape[1]
    return pl.pallas_call(
        prepare_kernel,
        out_shape=(
            jax.ShapeDtypeStruct((rows, 3 * BLK), BF16),
            jax.ShapeDtypeStruct((rows, edges), BF16),
            jax.ShapeDtypeStruct((edges, VECS), F32),
            jax.ShapeDtypeStruct(field.shape, BF16),
        ),
        in_specs=[SMEM, *(HBM,) * 5],
        out_specs=(VMEM,) * 4,
        scratch_shapes=[
            pltpu.VMEM(dst.shape, jnp.int32),
            pltpu.VMEM(far.shape, F32),
            pltpu.VMEM(wts.shape, F32),
            pltpu.VMEM(cols.shape, jnp.int32),
            pltpu.SemaphoreType.DMA((5,)),
        ],
        compiler_params=PARAMS,
        name="prepare",
    )(place, dst, far, wts, cols, field)


def send_out(even, first, last, picked, sent):
    sent = dict(zip(LINKS, sent, strict=True))
    sent[1, 0][...] = jnp.where(even, last, first)
    sent[1, 1][...] = jnp.where(even, first, last)
    for g, link in enumerate(FAR_LINKS):
        sent[link][:CAP, :] = picked[g * CAP : (g + 1) * CAP].astype(BF16)


def first_kernel(place_ref, field_ref, w0, w1, w2, w3, pick_mat_ref, *sent):
    rows = field_ref.shape[0]
    half = 2 * CAP
    lanes = lax.broadcasted_iota(jnp.int32, (1, half), 1)
    for i, (by, pair) in enumerate(zip(FAR, ((w0, w1), (w2, w3)), strict=True)):
        ahead, back = (w[:, i * half : (i + 1) * half] for w in pair)
        low = is_low(place_ref, by)
        ahead = jnp.where(low, turned(ahead), ahead)
        back = jnp.where(low, turned(back), back)
        wanted = jnp.where(lanes < CAP, ahead, back)
        column = as_columns(wanted.astype(F32))
        for b in range(rows // BLK):
            ids = lax.broadcasted_iota(jnp.int32, (half, BLK), 1) + b * BLK
            hot = jnp.where(column == ids.astype(F32), 1.0, 0.0).astype(BF16)
            pick_mat_ref[pl.ds(i * half, half), pl.ds(b * BLK, BLK)] = hot
    field = field_ref[...]
    picked = dot(pick_mat_ref[...], field, ((1,), (0,)))
    send_out(is_low(place_ref, 1), field[:BLK], field[rows - BLK :], picked, sent)


SENT = tuple(jax.ShapeDtypeStruct((BLK, VECS), BF16) for _ in LINKS)


def first(place, field, wanted):
    rows = field.shape[0]
    return pl.pallas_call(
        first_kernel,
        out_shape=(jax.ShapeDtypeStruct((PEERS * CAP, rows), BF16), *SENT),
        in_specs=[SMEM] + [VMEM] * 5,
        out_specs=(VMEM,) * 7,
        compiler_params=PARAMS,
        name="first",
    )(place, field, *wanted)


def advance(place_ref, band_ref, hot_ref, coef_ref, field_ref, prev_ref, got, scale, store):
    rows = field_ref.shape[0]
    count = rows // BLK
    even = is_low(place_ref, 1)
    got = dict(zip(LINKS, got, strict=True))
    low = jnp.where(even, got[1, 1][...], got[1, 0][...])
    high = jnp.where(even, got[1, 0][...], got[1, 1][...])
    far = jnp.concatenate([got[link][:CAP, :] for link in FAR_LINKS], axis=0)
    far = far.astype(F32) * coef_ref[...]
    far_high = far.astype(BF16)
    far_low = (far - far_high.astype(F32)).astype(BF16)
    far = jnp.concatenate([far_high, far_low], axis=1)
    for b in range(count):
        block = pl.ds(b * BLK, BLK)
        both = dot(hot_ref[block, :], far, ((1,), (0,)))
        total = both[:, :VECS] + both[:, VECS:]
        if b == 0:
            total += dot(band_ref[block, :BLK], low, ((1,), (0,)))
            total += dot(band_ref[block, BLK:], field_ref[: 2 * BLK, :], ((1,), (0,)))
        elif b == count - 1:
            total += dot(
                band_ref[block, : 2 * BLK], field_ref[rows - 2 * BLK :, :], ((1,), (0,))
            )
            total += dot(band_ref[block, 2 * BLK :], high, ((1,), (0,)))
        else:
            total += dot(
                band_ref[block, :], field_ref[pl.ds((b - 1) * BLK, 3 * BLK), :], ((1,), (0,))
            )
        value = total * scale
        if prev_ref is not None:
            value = value - prev_ref[block, :].astype(F32)
        store(block, value)
    return even


def step_kernel(scale, has_prev, has_next, *refs):
    place_ref, band_ref, hot_ref, coef_ref, pick_mat_ref, field_ref = refs[:6]
    refs = refs[6:]
    prev_ref = None
    if has_prev:
        prev_ref, refs = refs[0], refs[1:]
    got, refs = refs[:6], refs[6:]
    packed_ref, sent, next_refs = refs[0], refs[1:7], refs[7:]

    def store(block, value):
        if has_next:
            next_refs[0][block, :] = value
        packed_ref[block, :] = value.astype(BF16)

    even = advance(
        place_ref, band_ref, hot_ref, coef_ref, field_ref, prev_ref, got, scale, store
    )
    rows = field_ref.shape[0]
    picked = dot(pick_mat_ref[...], packed_ref[...], ((1,), (0,)))
    send_out(even, packed_ref[:BLK, :], packed_ref[rows - BLK :, :], picked, sent)


def step(scale, place, mats, field, prev, got, has_next=True):
    rows = field.shape[0]
    has_prev = prev is not None
    before = (prev,) if has_prev else ()
    return pl.pallas_call(
        lambda *refs: step_kernel(scale, has_prev, has_next, *refs),
        out_shape=(
            jax.ShapeDtypeStruct((rows, VECS), BF16),
            *SENT,
            *(jax.ShapeDtypeStruct((rows, VECS), F32),) * has_next,
        ),
        in_specs=[SMEM] + [VMEM] * (11 + len(before)),
        out_specs=(VMEM,) * (7 + has_next),
        compiler_params=PARAMS,
        name="step",
    )(place, *mats, field, *before, *got)


def last_kernel(scale, *refs):
    place_ref, band_ref, hot_ref, coef_ref, field_ref, prev_ref = refs[:6]
    got, (next_ref, gram_ref) = refs[6:12], refs[12:]

    def store(block, value):
        next_ref[block, :] = value

    advance(
        place_ref, band_ref, hot_ref, coef_ref, field_ref, prev_ref, got, scale, store
    )
    value = next_ref[...]
    gram_ref[...] = dot(value, value, ((0,), (0,)), lax.Precision.HIGHEST)


def last(scale, place, mats, field, prev, got):
    rows = field.shape[0]
    return pl.pallas_call(
        lambda *refs: last_kernel(scale, *refs),
        out_shape=(
            jax.ShapeDtypeStruct((rows, VECS), F32),
            jax.ShapeDtypeStruct((VECS, VECS), F32),
        ),
        in_specs=[SMEM] + [VMEM] * 11,
        out_specs=(VMEM, VMEM),
        compiler_params=PARAMS,
        name="last",
    )(place, *mats, field, prev, *got)


def total_of(terms):
    terms = list(terms)
    while len(terms) > 1:
        pairs = [terms[i] + terms[i + 1] for i in range(0, len(terms) - 1, 2)]
        terms = pairs + terms[len(terms) - len(terms) % 2 :]
    return terms[0]


def finish_kernel(scale, gram_ref, field_ref, out_ref, inverse_ref):
    width = 8
    shape = (width, VECS)
    panels = VECS // width
    ids = lax.broadcasted_iota(jnp.int32, shape, 0)
    lanes = lax.broadcasted_iota(jnp.int32, shape, 1)

    def spread(value):
        return jnp.broadcast_to(value, shape)

    left = [gram_ref[width * b : width * (b + 1), :] for b in range(panels)]
    right = [jnp.where(ids + width * b == lanes, 1.0, 0.0) for b in range(panels)]
    for p in range(panels):
        base = width * p
        columns = [spread(left[p][:, base + c : base + c + 1]) for c in range(width)]
        entry = {
            (i, c): spread(columns[c][i : i + 1, :]) for i in range(width) for c in range(i + 1)
        }
        inverse, l, n = [], {}, {}
        for j in range(width):
            inverse.append(1.0 / entry[j, j])
            for i in range(j + 1, width):
                l[i, j] = entry[i, j] * inverse[j]
            for c in range(j + 1, width):
                for i in range(c, width):
                    entry[i, c] = entry[i, c] - l[i, j] * entry[c, j]
        for j in range(width):
            for i in range(j + 1, width):
                n[i, j] = -total_of([l[i, j], *(l[i, m] * n[m, j] for m in range(j + 1, i))])
        factors = []
        for side in (left, right):
            raw = [spread(side[p][i : i + 1, :]) for i in range(width)]
            done = [total_of([raw[i], *(n[i, j] * raw[j] for j in range(i))]) for i in range(width)]
            if side is right:
                for i in range(width):
                    row = done[i] * (lax.rsqrt(entry[i, i]) * scale)
                    inverse_ref[base + i : base + i + 1, :] = row[:1, :]
            done = [d * v for d, v in zip(done, inverse)]
            factors.append(
                [
                    total_of([done[c], *(n[i, c] * done[i] for i in range(c + 1, width))])
                    for c in range(width)
                ]
            )
        for b in range(p + 1, panels):
            columns = [spread(left[b][:, base + c : base + c + 1]) for c in range(width)]
            for side, rows in zip((left, right), factors):
                side[b] = side[b] - total_of(c * r for c, r in zip(columns, rows))
    out_ref[...] = dot(field_ref[...], inverse_ref[...], ((1,), (1,)), lax.Precision.HIGHEST)


def finish(scale, gram, field):
    return pl.pallas_call(
        lambda *refs: finish_kernel(scale, *refs),
        out_shape=jax.ShapeDtypeStruct(field.shape, F32),
        in_specs=[VMEM] * 2,
        out_specs=VMEM,
        scratch_shapes=[pltpu.VMEM((VECS, VECS), F32)],
        compiler_params=PARAMS,
        name="finish",
    )(gram, field)


def summed(value, count):
    bits = [1 << i for i in range(count.bit_length() - 1)]
    stages = [bits[:1]] + [bits[i : i + 2] for i in range(1, len(bits), 2)]
    for stage in stages:
        masks = [stage[0]] if len(stage) == 1 else [*stage, stage[0] ^ stage[1]]
        total = value
        for mask in masks:
            total = total + lax.ppermute(value, AXES, [(i, i ^ mask) for i in range(count)])
        value = total
    return value


def local(start_basis, band_cols, band_wts, far_dst, far_src, far_wts):
    count = lax.axis_size(AXES)
    place = lax.axis_index(AXES)
    total_rows = start_basis.shape[0] * count

    def swap(value, by, odd):
        return lax.ppermute(value, AXES, swap_pairs(count, by, odd))

    def as_row(value):
        return value.reshape(1, -1)

    asked = as_row(far_src)
    wanted = [swap(asked, *link) for link in FAR_LINKS]
    here = place.astype(jnp.int32).reshape(1)
    band, hot, coef, field = prepare(
        here,
        as_row(far_dst),
        as_row(far_wts),
        jnp.transpose(band_wts, (1, 2, 0)),
        jnp.transpose(band_cols, (1, 2, 0)),
        start_basis,
    )
    wanted, band = lax.optimization_barrier((wanted, band))
    pick_mat, *sent = first(here, field, wanted)

    def exchange(sent):
        return [swap(v, *link) for v, link in zip(sent, LINKS, strict=True)]

    previous, packed = field, field
    mats = (band, hot, coef, pick_mat)
    got = exchange(sent)
    packed, *sent, current = step(1.0 / HALF_WIDTH, here, mats, packed, None, got)
    for _ in range(DEGREE - 3):
        got = exchange(sent)
        packed, *sent, following = step(2.0 / HALF_WIDTH, here, mats, packed, previous, got)
        previous, current = current, following
    got = exchange(sent)
    packed, *sent = step(2.0 / HALF_WIDTH, here, mats, packed, previous, got, has_next=False)
    previous = current
    got = exchange(sent)
    filtered, gram = last(2.0 / HALF_WIDTH, here, mats[:3], packed, previous, got)
    return finish(math.sqrt(total_rows), summed(gram, count), filtered)


def solution(mesh):
    placed = (
        P(AXES, None),
        P(AXES, None, None),
        P(AXES, None, None),
        P(AXES),
        P(AXES),
        P(AXES),
    )
    return jax.shard_map(
        local, mesh=mesh, in_specs=placed, out_specs=P(AXES, None), check_vma=False
    )
```

```python
import math

import jax
import jax.numpy as jnp
from jax import lax
from jax.experimental import pallas as pl
from jax.experimental.pallas import tpu as pltpu
from jax.sharding import PartitionSpec as P

VECS = 128
BLK = 128
KB = 8
PEERS = 4
CAP = 64
DEGREE = 8
HALF_WIDTH = 0.95
AXES = ("row", "snk")
FAR = (2, 4)
LINKS = ((4, 1), (2, 1), (1, 1), (4, 0), (2, 0), (1, 0))
FAR_LINKS = tuple((by, odd) for by in FAR for odd in (0, 1))
BF16 = jnp.bfloat16
F32 = jnp.float32
VMEM = pl.BlockSpec(memory_space=pltpu.VMEM)
HBM = pl.BlockSpec(memory_space=pltpu.HBM)
SMEM = pl.BlockSpec(memory_space=pltpu.SMEM)
PARAMS = pltpu.CompilerParams(vmem_limit_bytes=24 * 1024 * 1024)


def swap_pairs(count, by, odd):
    pairs = []
    for low in range(count):
        if (low // by) % 2 == odd:
            high = (low + by) % count
            pairs += [(low, high), (high, low)]
    return pairs


def split3(value):
    high = value.astype(BF16)
    rest = value - high.astype(F32)
    mid = rest.astype(BF16)
    low = (rest - mid.astype(F32)).astype(BF16)
    return high, mid, low


def stacked(value, height):
    parts = split3(value)
    pad = jnp.zeros((height - 3, value.shape[1]), BF16)
    return jnp.concatenate([*parts, pad], axis=0)


def dot(a, b, dims, precision=None):
    return lax.dot_general(
        a, b, (dims, ((), ())), precision=precision, preferred_element_type=F32
    )


def is_low(place_ref, by):
    return lax.rem(lax.div(place_ref[0], by), 2) == 0


def turned(row):
    half = row.shape[1] // 2
    return jnp.concatenate([row[:, half:], row[:, :half]], axis=1)


def by_link(place_ref, row):
    parts = []
    for i, by in enumerate(FAR):
        pair = row[:, 2 * CAP * i : 2 * CAP * (i + 1)]
        parts.append(jnp.where(is_low(place_ref, by), pair, turned(pair)))
    return jnp.concatenate(parts, axis=1)


def as_rows(row):
    return jnp.concatenate([jnp.broadcast_to(row, (16, row.shape[1])).astype(BF16)] * (BLK // 16), axis=0)


def as_columns(row):
    return jnp.broadcast_to(row, (row.shape[1], row.shape[1])).T


def prepare_kernel(
    place_ref,
    dst_any,
    far_any,
    wts_any,
    cols_any,
    field_any,
    band_ref,
    hot_ref,
    coef_ref,
    field_ref,
    dst_ref,
    far_ref,
    wts_ref,
    cols_ref,
    sems,
):
    copies = [
        pltpu.make_async_copy(source, target, sems.at[i])
        for i, (source, target) in enumerate(
            (
                (dst_any, dst_ref),
                (far_any, far_ref),
                (wts_any, wts_ref),
                (cols_any, cols_ref),
                (field_any, field_ref),
            )
        )
    ]
    for copy in copies:
        copy.start()
    copies[0].wait()
    copies[1].wait()
    rows = cols_ref.shape[2]
    edges = dst_ref.shape[1]
    dst = by_link(place_ref, dst_ref[...])
    far = by_link(place_ref, far_ref[...])
    one, zero = jnp.ones((), BF16), jnp.zeros((), BF16)
    ids = lax.broadcasted_iota(jnp.int32, (BLK, edges), 0).astype(F32).astype(BF16)
    in_block = jnp.where(ids == as_rows(lax.rem(dst, BLK).astype(F32)), one, zero)
    owner = lax.div(dst, BLK)
    for b in range(rows // BLK):
        hot_ref[pl.ds(b * BLK, BLK), :] = in_block * as_rows(jnp.where(owner == b, 1.0, 0.0))
    hot = hot_ref[...]
    degree = jnp.sum(dot(stacked(far, 16), hot, ((1,), (1,))), axis=0, keepdims=True)
    copies[2].wait()
    for o in range(3):
        degree = degree + jnp.sum(wts_ref[o], axis=0, keepdims=True)
    at_edge = jnp.sum(dot(stacked(degree, 16), hot, ((1,), (0,))), axis=0, keepdims=True)
    far_coef = far / at_edge
    for i in range(edges // BLK):
        coef_ref[pl.ds(i * BLK, BLK), :] = as_columns(far_coef[:, i * BLK : (i + 1) * BLK])
    copies[3].wait()
    ids = ids[:, :BLK]
    for b in range(rows // BLK):
        block = pl.ds(b * BLK, BLK)
        degree_b = degree[:, b * BLK : (b + 1) * BLK]
        for o in range(3):
            cols = cols_ref[o, :, block].astype(F32)
            coef = wts_ref[o, :, block] / degree_b
            dense = jnp.zeros((BLK, BLK), BF16)
            for k in range(KB):
                here = ids == as_rows(cols[k : k + 1, :])
                dense = jnp.where(here, as_rows(coef[k : k + 1, :]), dense)
            band_ref[block, pl.ds(o * BLK, BLK)] = dense.T
    copies[4].wait()


def prepare(place, dst, far, wts, cols, field):
    rows, edges = cols.shape[2], dst.shape[1]
    return pl.pallas_call(
        prepare_kernel,
        out_shape=(
            jax.ShapeDtypeStruct((rows, 3 * BLK), BF16),
            jax.ShapeDtypeStruct((rows, edges), BF16),
            jax.ShapeDtypeStruct((edges, VECS), F32),
            jax.ShapeDtypeStruct(field.shape, BF16),
        ),
        in_specs=[SMEM, *(HBM,) * 5],
        out_specs=(VMEM,) * 4,
        scratch_shapes=[
            pltpu.VMEM(dst.shape, jnp.int32),
            pltpu.VMEM(far.shape, F32),
            pltpu.VMEM(wts.shape, F32),
            pltpu.VMEM(cols.shape, jnp.int32),
            pltpu.SemaphoreType.DMA((5,)),
        ],
        compiler_params=PARAMS,
        name="prepare",
    )(place, dst, far, wts, cols, field)


def send_out(even, first, last, picked, sent):
    sent = dict(zip(LINKS, sent, strict=True))
    sent[1, 0][...] = jnp.where(even, last, first)
    sent[1, 1][...] = jnp.where(even, first, last)
    for g, link in enumerate(FAR_LINKS):
        sent[link][:CAP, :] = picked[g * CAP : (g + 1) * CAP].astype(BF16)


def first_kernel(place_ref, field_ref, w0, w1, w2, w3, pick_mat_ref, *sent):
    rows = field_ref.shape[0]
    half = 2 * CAP
    lanes = lax.broadcasted_iota(jnp.int32, (1, half), 1)
    one, zero = jnp.ones((), BF16), jnp.zeros((), BF16)
    for i, (by, pair) in enumerate(zip(FAR, ((w0, w1), (w2, w3)), strict=True)):
        ahead, back = (w[:, i * half : (i + 1) * half] for w in pair)
        low = is_low(place_ref, by)
        ahead = jnp.where(low, turned(ahead), ahead)
        back = jnp.where(low, turned(back), back)
        wanted = jnp.where(lanes < CAP, ahead, back)
        column = as_columns(lax.rem(wanted, BLK).astype(F32)).astype(BF16)
        owner = as_columns(lax.div(wanted, BLK).astype(F32)).astype(BF16)
        ids = lax.broadcasted_iota(jnp.int32, (half, BLK), 1).astype(F32).astype(BF16)
        in_block = jnp.where(column == ids, one, zero)
        for b in range(rows // BLK):
            hot = jnp.where(owner == jnp.full((), b, BF16), in_block, zero)
            pick_mat_ref[pl.ds(i * half, half), pl.ds(b * BLK, BLK)] = hot
    field = field_ref[...]
    picked = dot(pick_mat_ref[...], field, ((1,), (0,)))
    send_out(is_low(place_ref, 1), field[:BLK], field[rows - BLK :], picked, sent)


SENT = tuple(jax.ShapeDtypeStruct((BLK, VECS), BF16) for _ in LINKS)


def first(place, field, wanted):
    rows = field.shape[0]
    return pl.pallas_call(
        first_kernel,
        out_shape=(jax.ShapeDtypeStruct((PEERS * CAP, rows), BF16), *SENT),
        in_specs=[SMEM] + [VMEM] * 5,
        out_specs=(VMEM,) * 7,
        compiler_params=PARAMS,
        name="first",
    )(place, field, *wanted)


def advance(place_ref, band_ref, hot_ref, coef_ref, field_ref, prev_ref, got, scale, store):
    rows = field_ref.shape[0]
    count = rows // BLK
    even = is_low(place_ref, 1)
    got = dict(zip(LINKS, got, strict=True))
    low = jnp.where(even, got[1, 1][...], got[1, 0][...])
    high = jnp.where(even, got[1, 0][...], got[1, 1][...])
    far = jnp.concatenate([got[link][:CAP, :] for link in FAR_LINKS], axis=0)
    far = far.astype(F32) * coef_ref[...]
    far_high = far.astype(BF16)
    far_low = (far - far_high.astype(F32)).astype(BF16)
    far = jnp.concatenate([far_high, far_low], axis=1)
    for b in range(count):
        block = pl.ds(b * BLK, BLK)
        both = dot(hot_ref[block, :], far, ((1,), (0,)))
        total = both[:, :VECS] + both[:, VECS:]
        if b == 0:
            total += dot(band_ref[block, :BLK], low, ((1,), (0,)))
            total += dot(band_ref[block, BLK:], field_ref[: 2 * BLK, :], ((1,), (0,)))
        elif b == count - 1:
            total += dot(
                band_ref[block, : 2 * BLK], field_ref[rows - 2 * BLK :, :], ((1,), (0,))
            )
            total += dot(band_ref[block, 2 * BLK :], high, ((1,), (0,)))
        else:
            total += dot(
                band_ref[block, :], field_ref[pl.ds((b - 1) * BLK, 3 * BLK), :], ((1,), (0,))
            )
        value = total * scale
        if prev_ref is not None:
            value = value - prev_ref[block, :].astype(F32)
        store(block, value)
    return even


def step_kernel(scale, has_prev, has_next, *refs):
    place_ref, band_ref, hot_ref, coef_ref, pick_mat_ref, field_ref = refs[:6]
    refs = refs[6:]
    prev_ref = None
    if has_prev:
        prev_ref, refs = refs[0], refs[1:]
    got, refs = refs[:6], refs[6:]
    packed_ref, sent, next_refs = refs[0], refs[1:7], refs[7:]

    def store(block, value):
        if has_next:
            next_refs[0][block, :] = value
        packed_ref[block, :] = value.astype(BF16)

    even = advance(
        place_ref, band_ref, hot_ref, coef_ref, field_ref, prev_ref, got, scale, store
    )
    rows = field_ref.shape[0]
    picked = dot(pick_mat_ref[...], packed_ref[...], ((1,), (0,)))
    send_out(even, packed_ref[:BLK, :], packed_ref[rows - BLK :, :], picked, sent)


def step(scale, place, mats, field, prev, got, has_next=True):
    rows = field.shape[0]
    has_prev = prev is not None
    before = (prev,) if has_prev else ()
    return pl.pallas_call(
        lambda *refs: step_kernel(scale, has_prev, has_next, *refs),
        out_shape=(
            jax.ShapeDtypeStruct((rows, VECS), BF16),
            *SENT,
            *(jax.ShapeDtypeStruct((rows, VECS), F32),) * has_next,
        ),
        in_specs=[SMEM] + [VMEM] * (11 + len(before)),
        out_specs=(VMEM,) * (7 + has_next),
        compiler_params=PARAMS,
        name="step",
    )(place, *mats, field, *before, *got)


def last_kernel(scale, *refs):
    place_ref, band_ref, hot_ref, coef_ref, field_ref, prev_ref = refs[:6]
    got, (next_ref, gram_ref) = refs[6:12], refs[12:]

    def store(block, value):
        next_ref[block, :] = value

    advance(
        place_ref, band_ref, hot_ref, coef_ref, field_ref, prev_ref, got, scale, store
    )
    value = next_ref[...]
    gram_ref[...] = dot(value, value, ((0,), (0,)), lax.Precision.HIGHEST)


def last(scale, place, mats, field, prev, got):
    rows = field.shape[0]
    return pl.pallas_call(
        lambda *refs: last_kernel(scale, *refs),
        out_shape=(
            jax.ShapeDtypeStruct((rows, VECS), F32),
            jax.ShapeDtypeStruct((VECS, VECS), F32),
        ),
        in_specs=[SMEM] + [VMEM] * 11,
        out_specs=(VMEM, VMEM),
        compiler_params=PARAMS,
        name="last",
    )(place, *mats, field, prev, *got)


def total_of(terms):
    terms = list(terms)
    while len(terms) > 1:
        pairs = [terms[i] + terms[i + 1] for i in range(0, len(terms) - 1, 2)]
        terms = pairs + terms[len(terms) - len(terms) % 2 :]
    return terms[0]


def finish_kernel(scale, gram_ref, field_ref, out_ref, inverse_ref):
    width = 8
    shape = (width, VECS)
    panels = VECS // width
    ids = lax.broadcasted_iota(jnp.int32, shape, 0)
    lanes = lax.broadcasted_iota(jnp.int32, shape, 1)

    def spread(value):
        return jnp.broadcast_to(value, shape)

    left = [gram_ref[width * b : width * (b + 1), :] for b in range(panels)]
    right = [jnp.where(ids + width * b == lanes, 1.0, 0.0) for b in range(panels)]
    for p in range(panels):
        base = width * p
        columns = [spread(left[p][:, base + c : base + c + 1]) for c in range(width)]
        entry = {
            (i, c): spread(columns[c][i : i + 1, :]) for i in range(width) for c in range(i + 1)
        }
        inverse, l, n = [], {}, {}
        for j in range(width):
            inverse.append(1.0 / entry[j, j])
            for i in range(j + 1, width):
                l[i, j] = entry[i, j] * inverse[j]
            for c in range(j + 1, width):
                for i in range(c, width):
                    entry[i, c] = entry[i, c] - l[i, j] * entry[c, j]
        for j in range(width):
            for i in range(j + 1, width):
                n[i, j] = -total_of([l[i, j], *(l[i, m] * n[m, j] for m in range(j + 1, i))])
        factors = []
        for side in (left, right):
            raw = [spread(side[p][i : i + 1, :]) for i in range(width)]
            done = [total_of([raw[i], *(n[i, j] * raw[j] for j in range(i))]) for i in range(width)]
            if side is right:
                for i in range(width):
                    row = done[i] * (lax.rsqrt(entry[i, i]) * scale)
                    inverse_ref[base + i : base + i + 1, :] = row[:1, :]
            done = [d * v for d, v in zip(done, inverse)]
            factors.append(
                [
                    total_of([done[c], *(n[i, c] * done[i] for i in range(c + 1, width))])
                    for c in range(width)
                ]
            )
        for b in range(p + 1, panels):
            columns = [spread(left[b][:, base + c : base + c + 1]) for c in range(width)]
            for side, rows in zip((left, right), factors):
                side[b] = side[b] - total_of(c * r for c, r in zip(columns, rows))
    out_ref[...] = dot(field_ref[...], inverse_ref[...], ((1,), (1,)), lax.Precision.HIGHEST)


def finish(scale, gram, field):
    return pl.pallas_call(
        lambda *refs: finish_kernel(scale, *refs),
        out_shape=jax.ShapeDtypeStruct(field.shape, F32),
        in_specs=[VMEM] * 2,
        out_specs=VMEM,
        scratch_shapes=[pltpu.VMEM((VECS, VECS), F32)],
        compiler_params=PARAMS,
        name="finish",
    )(gram, field)


def summed(value, count):
    bits = [1 << i for i in range(count.bit_length() - 1)]
    stages = [bits[:1]] + [bits[i : i + 2] for i in range(1, len(bits), 2)]
    for stage in stages:
        masks = [stage[0]] if len(stage) == 1 else [*stage, stage[0] ^ stage[1]]
        total = value
        for mask in masks:
            total = total + lax.ppermute(value, AXES, [(i, i ^ mask) for i in range(count)])
        value = total
    return value


def local(start_basis, band_cols, band_wts, far_dst, far_src, far_wts):
    count = lax.axis_size(AXES)
    place = lax.axis_index(AXES)
    total_rows = start_basis.shape[0] * count

    def swap(value, by, odd):
        return lax.ppermute(value, AXES, swap_pairs(count, by, odd))

    def as_row(value):
        return value.reshape(1, -1)

    asked = as_row(far_src)
    wanted = [swap(asked, *link) for link in FAR_LINKS]
    here = place.astype(jnp.int32).reshape(1)
    band, hot, coef, field = prepare(
        here,
        *(
            pltpu.with_memory_space_constraint(v, pltpu.HBM)
            for v in (
                as_row(far_dst),
                as_row(far_wts),
                jnp.transpose(band_wts, (1, 2, 0)),
                jnp.transpose(band_cols, (1, 2, 0)),
                start_basis,
            )
        ),
    )
    wanted, band = lax.optimization_barrier((wanted, band))
    pick_mat, *sent = first(here, field, wanted)

    def exchange(sent):
        return [swap(v, *link) for v, link in zip(sent, LINKS, strict=True)]

    previous, packed = field, field
    mats = (band, hot, coef, pick_mat)
    got = exchange(sent)
    packed, *sent, current = step(1.0 / HALF_WIDTH, here, mats, packed, None, got)
    for _ in range(DEGREE - 3):
        got = exchange(sent)
        packed, *sent, following = step(2.0 / HALF_WIDTH, here, mats, packed, previous, got)
        previous, current = current, following
    got = exchange(sent)
    packed, *sent = step(2.0 / HALF_WIDTH, here, mats, packed, previous, got, has_next=False)
    previous = current
    got = exchange(sent)
    filtered, gram = last(2.0 / HALF_WIDTH, here, mats[:3], packed, previous, got)
    return finish(math.sqrt(total_rows), summed(gram, count), filtered)


def solution(mesh):
    placed = (
        P(AXES, None),
        P(AXES, None, None),
        P(AXES, None, None),
        P(AXES),
        P(AXES),
        P(AXES),
    )
    return jax.shard_map(
        local, mesh=mesh, in_specs=placed, out_specs=P(AXES, None), check_vma=False
    )
```

```python
import math

import jax
import jax.numpy as jnp
from jax import lax
from jax.experimental import pallas as pl
from jax.experimental.pallas import tpu as pltpu
from jax.sharding import PartitionSpec as P

VECS = 128
BLK = 128
KB = 8
PEERS = 4
CAP = 64
DEGREE = 8
HALF_WIDTH = 0.95
AXES = ("row", "snk")
FAR = (2, 4)
LINKS = ((4, 1), (2, 1), (1, 1), (4, 0), (2, 0), (1, 0))
FAR_LINKS = tuple((by, odd) for by in FAR for odd in (0, 1))
BF16 = jnp.bfloat16
F32 = jnp.float32
VMEM = pl.BlockSpec(memory_space=pltpu.VMEM)
HBM = pl.BlockSpec(memory_space=pltpu.HBM)
SMEM = pl.BlockSpec(memory_space=pltpu.SMEM)
PARAMS = pltpu.CompilerParams(vmem_limit_bytes=24 * 1024 * 1024)


def swap_pairs(count, by, odd):
    pairs = []
    for low in range(count):
        if (low // by) % 2 == odd:
            high = (low + by) % count
            pairs += [(low, high), (high, low)]
    return pairs


def split3(value):
    high = value.astype(BF16)
    rest = value - high.astype(F32)
    mid = rest.astype(BF16)
    low = (rest - mid.astype(F32)).astype(BF16)
    return high, mid, low


def stacked(value, height):
    parts = split3(value)
    pad = jnp.zeros((height - 3, value.shape[1]), BF16)
    return jnp.concatenate([*parts, pad], axis=0)


def dot(a, b, dims, precision=None):
    return lax.dot_general(
        a, b, (dims, ((), ())), precision=precision, preferred_element_type=F32
    )


def is_low(place_ref, by):
    return lax.rem(lax.div(place_ref[0], by), 2) == 0


def turned(row):
    half = row.shape[1] // 2
    return jnp.concatenate([row[:, half:], row[:, :half]], axis=1)


def by_link(place_ref, row):
    parts = []
    for i, by in enumerate(FAR):
        pair = row[:, 2 * CAP * i : 2 * CAP * (i + 1)]
        parts.append(jnp.where(is_low(place_ref, by), pair, turned(pair)))
    return jnp.concatenate(parts, axis=1)


def as_rows(row):
    return jnp.concatenate([jnp.broadcast_to(row, (16, row.shape[1])).astype(BF16)] * (BLK // 16), axis=0)


def as_columns(row):
    return jnp.broadcast_to(row, (row.shape[1], row.shape[1])).T


def prepare_kernel(
    place_ref,
    dst_any,
    far_any,
    wts_any,
    cols_any,
    field_any,
    band_ref,
    hot_ref,
    coef_ref,
    field_ref,
    dst_ref,
    far_ref,
    wts_ref,
    cols_ref,
    sems,
):
    copies = [
        pltpu.make_async_copy(source, target, sems.at[i])
        for i, (source, target) in enumerate(
            (
                (dst_any, dst_ref),
                (far_any, far_ref),
                (wts_any, wts_ref),
                (cols_any, cols_ref),
                (field_any, field_ref),
            )
        )
    ]
    for copy in copies:
        copy.start()
    copies[0].wait()
    copies[1].wait()
    rows = cols_ref.shape[2]
    edges = dst_ref.shape[1]
    dst = by_link(place_ref, dst_ref[...])
    far = by_link(place_ref, far_ref[...])
    one, zero = jnp.ones((), BF16), jnp.zeros((), BF16)
    ids = lax.broadcasted_iota(jnp.int32, (BLK, edges), 0).astype(F32).astype(BF16)
    in_block = jnp.where(ids == as_rows(lax.rem(dst, BLK).astype(F32)), one, zero)
    owner = lax.div(dst, BLK)
    for b in range(rows // BLK):
        hot_ref[pl.ds(b * BLK, BLK), :] = in_block * as_rows(jnp.where(owner == b, 1.0, 0.0))
    hot = hot_ref[...]
    degree = jnp.sum(dot(stacked(far, 16), hot, ((1,), (1,))), axis=0, keepdims=True)
    copies[2].wait()
    for o in range(3):
        degree = degree + jnp.sum(wts_ref[o], axis=0, keepdims=True)
    at_edge = jnp.sum(dot(stacked(degree, 16), hot, ((1,), (0,))), axis=0, keepdims=True)
    far_coef = far / at_edge
    for i in range(edges // BLK):
        coef_ref[pl.ds(i * BLK, BLK), :] = as_columns(far_coef[:, i * BLK : (i + 1) * BLK])
    copies[3].wait()
    ids = ids[:, :BLK]
    for b in range(rows // BLK):
        block = pl.ds(b * BLK, BLK)
        degree_b = degree[:, b * BLK : (b + 1) * BLK]
        for o in range(3):
            cols = cols_ref[o, :, block].astype(F32)
            coef = wts_ref[o, :, block] / degree_b
            dense = jnp.zeros((BLK, BLK), BF16)
            for k in range(KB):
                here = ids == as_rows(cols[k : k + 1, :])
                dense = jnp.where(here, as_rows(coef[k : k + 1, :]), dense)
            band_ref[block, pl.ds(o * BLK, BLK)] = dense.T
    copies[4].wait()


def prepare(place, dst, far, wts, cols, field):
    rows, edges = cols.shape[2], dst.shape[1]
    return pl.pallas_call(
        prepare_kernel,
        out_shape=(
            jax.ShapeDtypeStruct((rows, 3 * BLK), BF16),
            jax.ShapeDtypeStruct((rows, edges), BF16),
            jax.ShapeDtypeStruct((edges, VECS), F32),
            jax.ShapeDtypeStruct(field.shape, BF16),
        ),
        in_specs=[SMEM, *(HBM,) * 5],
        out_specs=(VMEM,) * 4,
        scratch_shapes=[
            pltpu.VMEM(dst.shape, jnp.int32),
            pltpu.VMEM(far.shape, F32),
            pltpu.VMEM(wts.shape, F32),
            pltpu.VMEM(cols.shape, jnp.int32),
            pltpu.SemaphoreType.DMA((5,)),
        ],
        compiler_params=PARAMS,
        name="prepare",
    )(place, dst, far, wts, cols, field)


def send_out(even, first, last, picked, sent):
    sent = dict(zip(LINKS, sent, strict=True))
    sent[1, 0][...] = jnp.where(even, last, first)
    sent[1, 1][...] = jnp.where(even, first, last)
    for g, link in enumerate(FAR_LINKS):
        sent[link][:CAP, :] = picked[g * CAP : (g + 1) * CAP].astype(BF16)


def first_kernel(place_ref, field_ref, w0, w1, w2, w3, pick_mat_ref, *sent):
    rows = field_ref.shape[0]
    half = 2 * CAP
    lanes = lax.broadcasted_iota(jnp.int32, (1, half), 1)
    one, zero = jnp.ones((), BF16), jnp.zeros((), BF16)
    for i, (by, pair) in enumerate(zip(FAR, ((w0, w1), (w2, w3)), strict=True)):
        ahead, back = (w[:, i * half : (i + 1) * half] for w in pair)
        low = is_low(place_ref, by)
        ahead = jnp.where(low, turned(ahead), ahead)
        back = jnp.where(low, turned(back), back)
        wanted = jnp.where(lanes < CAP, ahead, back)
        column = as_columns(lax.rem(wanted, BLK).astype(F32)).astype(BF16)
        owner = as_columns(lax.div(wanted, BLK).astype(F32)).astype(BF16)
        ids = lax.broadcasted_iota(jnp.int32, (half, BLK), 1).astype(F32).astype(BF16)
        in_block = jnp.where(column == ids, one, zero)
        for b in range(rows // BLK):
            hot = jnp.where(owner == jnp.full((), b, BF16), in_block, zero)
            pick_mat_ref[pl.ds(i * half, half), pl.ds(b * BLK, BLK)] = hot
    field = field_ref[...]
    picked = dot(pick_mat_ref[...], field, ((1,), (0,)))
    send_out(is_low(place_ref, 1), field[:BLK], field[rows - BLK :], picked, sent)


SENT = tuple(jax.ShapeDtypeStruct((BLK, VECS), BF16) for _ in LINKS)


def first(place, field, wanted):
    rows = field.shape[0]
    return pl.pallas_call(
        first_kernel,
        out_shape=(jax.ShapeDtypeStruct((PEERS * CAP, rows), BF16), *SENT),
        in_specs=[SMEM] + [VMEM] * 5,
        out_specs=(VMEM,) * 7,
        compiler_params=PARAMS,
        name="first",
    )(place, field, *wanted)


def advance(place_ref, band_ref, hot_ref, coef_ref, field_ref, prev_ref, got, scale, store):
    rows = field_ref.shape[0]
    count = rows // BLK
    even = is_low(place_ref, 1)
    got = dict(zip(LINKS, got, strict=True))
    low = jnp.where(even, got[1, 1][...], got[1, 0][...])
    high = jnp.where(even, got[1, 0][...], got[1, 1][...])
    far = jnp.concatenate([got[link][:CAP, :] for link in FAR_LINKS], axis=0)
    far = far.astype(F32) * coef_ref[...]
    far_high = far.astype(BF16)
    far_low = (far - far_high.astype(F32)).astype(BF16)
    far = jnp.concatenate([far_high, far_low], axis=1)
    for b in range(count):
        block = pl.ds(b * BLK, BLK)
        both = dot(hot_ref[block, :], far, ((1,), (0,)))
        total = both[:, :VECS] + both[:, VECS:]
        if b == 0:
            total += dot(band_ref[block, :BLK], low, ((1,), (0,)))
            total += dot(band_ref[block, BLK:], field_ref[: 2 * BLK, :], ((1,), (0,)))
        elif b == count - 1:
            total += dot(
                band_ref[block, : 2 * BLK], field_ref[rows - 2 * BLK :, :], ((1,), (0,))
            )
            total += dot(band_ref[block, 2 * BLK :], high, ((1,), (0,)))
        else:
            total += dot(
                band_ref[block, :], field_ref[pl.ds((b - 1) * BLK, 3 * BLK), :], ((1,), (0,))
            )
        value = total * scale
        if prev_ref is not None:
            value = value - prev_ref[block, :].astype(F32)
        store(block, value)
    return even


def step_kernel(scale, has_prev, has_next, *refs):
    place_ref, band_ref, hot_ref, coef_ref, pick_mat_ref, field_ref = refs[:6]
    refs = refs[6:]
    prev_ref = None
    if has_prev:
        prev_ref, refs = refs[0], refs[1:]
    got, refs = refs[:6], refs[6:]
    packed_ref, sent, next_refs = refs[0], refs[1:7], refs[7:]

    def store(block, value):
        if has_next:
            next_refs[0][block, :] = value
        packed_ref[block, :] = value.astype(BF16)

    even = advance(
        place_ref, band_ref, hot_ref, coef_ref, field_ref, prev_ref, got, scale, store
    )
    rows = field_ref.shape[0]
    picked = dot(pick_mat_ref[...], packed_ref[...], ((1,), (0,)))
    send_out(even, packed_ref[:BLK, :], packed_ref[rows - BLK :, :], picked, sent)


def step(scale, place, mats, field, prev, got, has_next=True):
    rows = field.shape[0]
    has_prev = prev is not None
    before = (prev,) if has_prev else ()
    return pl.pallas_call(
        lambda *refs: step_kernel(scale, has_prev, has_next, *refs),
        out_shape=(
            jax.ShapeDtypeStruct((rows, VECS), BF16),
            *SENT,
            *(jax.ShapeDtypeStruct((rows, VECS), F32),) * has_next,
        ),
        in_specs=[SMEM] + [VMEM] * (11 + len(before)),
        out_specs=(VMEM,) * (7 + has_next),
        compiler_params=PARAMS,
        name="step",
    )(place, *mats, field, *before, *got)


def last_kernel(scale, *refs):
    place_ref, band_ref, hot_ref, coef_ref, field_ref, prev_ref = refs[:6]
    got, (next_ref, kept_ref, sent_ref) = refs[6:12], refs[12:]

    def store(block, value):
        next_ref[block, :] = value

    advance(
        place_ref, band_ref, hot_ref, coef_ref, field_ref, prev_ref, got, scale, store
    )
    value = next_ref[...]
    gram = dot(value, value, ((0,), (0,)), lax.Precision.HIGHEST)
    half = VECS // 2
    low = is_low(place_ref, 1)
    kept_ref[...] = jnp.where(low, gram[:half], gram[half:])
    sent_ref[...] = jnp.where(low, gram[half:], gram[:half])


def last(scale, place, mats, field, prev, got):
    rows = field.shape[0]
    return pl.pallas_call(
        lambda *refs: last_kernel(scale, *refs),
        out_shape=(
            jax.ShapeDtypeStruct((rows, VECS), F32),
            *(jax.ShapeDtypeStruct((VECS // 2, VECS), F32),) * 2,
        ),
        in_specs=[SMEM] + [VMEM] * 11,
        out_specs=(VMEM,) * 3,
        compiler_params=PARAMS,
        name="last",
    )(place, *mats, field, prev, *got)


def total_of(terms):
    terms = list(terms)
    while len(terms) > 1:
        pairs = [terms[i] + terms[i + 1] for i in range(0, len(terms) - 1, 2)]
        terms = pairs + terms[len(terms) - len(terms) % 2 :]
    return terms[0]


def finish_kernel(scale, place_ref, own_ref, other_ref, field_ref, out_ref, inverse_ref):
    width = 8
    shape = (width, VECS)
    panels = VECS // width
    ids = lax.broadcasted_iota(jnp.int32, shape, 0)
    lanes = lax.broadcasted_iota(jnp.int32, shape, 1)

    def spread(value):
        return jnp.broadcast_to(value, shape)

    low = is_low(place_ref, 1)
    gram = jnp.concatenate(
        [
            jnp.where(low, own_ref[...], other_ref[...]),
            jnp.where(low, other_ref[...], own_ref[...]),
        ],
        axis=0,
    )
    left = [gram[width * b : width * (b + 1), :] for b in range(panels)]
    right = [jnp.where(ids + width * b == lanes, 1.0, 0.0) for b in range(panels)]
    for p in range(panels):
        base = width * p
        columns = [spread(left[p][:, base + c : base + c + 1]) for c in range(width)]
        entry = {
            (i, c): spread(columns[c][i : i + 1, :]) for i in range(width) for c in range(i + 1)
        }
        inverse, l, n = [], {}, {}
        for j in range(width):
            inverse.append(1.0 / entry[j, j])
            for i in range(j + 1, width):
                l[i, j] = entry[i, j] * inverse[j]
            for c in range(j + 1, width):
                for i in range(c, width):
                    entry[i, c] = entry[i, c] - l[i, j] * entry[c, j]
        for j in range(width):
            for i in range(j + 1, width):
                n[i, j] = -total_of([l[i, j], *(l[i, m] * n[m, j] for m in range(j + 1, i))])
        factors = []
        for side in (left, right):
            raw = [spread(side[p][i : i + 1, :]) for i in range(width)]
            done = [total_of([raw[i], *(n[i, j] * raw[j] for j in range(i))]) for i in range(width)]
            if side is right:
                for i in range(width):
                    row = done[i] * (lax.rsqrt(entry[i, i]) * scale)
                    inverse_ref[base + i : base + i + 1, :] = row[:1, :]
            done = [d * v for d, v in zip(done, inverse)]
            factors.append(
                [
                    total_of([done[c], *(n[i, c] * done[i] for i in range(c + 1, width))])
                    for c in range(width)
                ]
            )
        for b in range(p + 1, panels):
            columns = [spread(left[b][:, base + c : base + c + 1]) for c in range(width)]
            for side, rows in zip((left, right), factors):
                side[b] = side[b] - total_of(c * r for c, r in zip(columns, rows))
    out_ref[...] = dot(field_ref[...], inverse_ref[...], ((1,), (1,)), lax.Precision.HIGHEST)


def finish(scale, place, halves, field):
    return pl.pallas_call(
        lambda *refs: finish_kernel(scale, *refs),
        out_shape=jax.ShapeDtypeStruct(field.shape, F32),
        in_specs=[SMEM] + [VMEM] * 3,
        out_specs=VMEM,
        scratch_shapes=[pltpu.VMEM((VECS, VECS), F32)],
        compiler_params=PARAMS,
        name="finish",
    )(place, *halves, field)


def summed(kept, sent, count):
    def swapped(value, mask):
        return lax.ppermute(value, AXES, [(i, i ^ mask) for i in range(count)])

    bits = [1 << i for i in range(1, count.bit_length() - 1)]
    half = kept + swapped(sent, 1)
    for i in range(0, len(bits), 2):
        stage = bits[i : i + 2]
        masks = stage if len(stage) == 1 else [*stage, stage[0] ^ stage[1]]
        half = sum((swapped(half, mask) for mask in masks), half)
    return half, swapped(half, 1)


def local(start_basis, band_cols, band_wts, far_dst, far_src, far_wts):
    count = lax.axis_size(AXES)
    place = lax.axis_index(AXES)
    total_rows = start_basis.shape[0] * count

    def swap(value, by, odd):
        return lax.ppermute(value, AXES, swap_pairs(count, by, odd))

    def as_row(value):
        return value.reshape(1, -1)

    asked = as_row(far_src)
    wanted = [swap(asked, *link) for link in FAR_LINKS]
    here = place.astype(jnp.int32).reshape(1)
    band, hot, coef, field = prepare(
        here,
        *(
            pltpu.with_memory_space_constraint(v, pltpu.HBM)
            for v in (
                as_row(far_dst),
                as_row(far_wts),
                jnp.transpose(band_wts, (1, 2, 0)),
                jnp.transpose(band_cols, (1, 2, 0)),
                start_basis,
            )
        ),
    )
    wanted, band = lax.optimization_barrier((wanted, band))
    pick_mat, *sent = first(here, field, wanted)

    def exchange(sent):
        return [swap(v, *link) for v, link in zip(sent, LINKS, strict=True)]

    previous, packed = field, field
    mats = (band, hot, coef, pick_mat)
    got = exchange(sent)
    packed, *sent, current = step(1.0 / HALF_WIDTH, here, mats, packed, None, got)
    for _ in range(DEGREE - 3):
        got = exchange(sent)
        packed, *sent, following = step(2.0 / HALF_WIDTH, here, mats, packed, previous, got)
        previous, current = current, following
    got = exchange(sent)
    packed, *sent = step(2.0 / HALF_WIDTH, here, mats, packed, previous, got, has_next=False)
    previous = current
    got = exchange(sent)
    filtered, kept, sent = last(2.0 / HALF_WIDTH, here, mats[:3], packed, previous, got)
    return finish(math.sqrt(total_rows), here, summed(kept, sent, count), filtered)


def solution(mesh):
    placed = (
        P(AXES, None),
        P(AXES, None, None),
        P(AXES, None, None),
        P(AXES),
        P(AXES),
        P(AXES),
    )
    return jax.shard_map(
        local, mesh=mesh, in_specs=placed, out_specs=P(AXES, None), check_vma=False
    )
```

```python
import math

import jax
import jax.numpy as jnp
from jax import lax
from jax.experimental import pallas as pl
from jax.experimental.pallas import tpu as pltpu
from jax.sharding import PartitionSpec as P

VECS = 128
BLK = 128
KB = 8
PEERS = 4
CAP = 64
DEGREE = 8
HALF_WIDTH = 0.95
AXES = ("row", "snk")
FAR = (2, 4)
LINKS = ((4, 1), (2, 1), (1, 1), (4, 0), (2, 0), (1, 0))
FAR_LINKS = tuple((by, odd) for by in FAR for odd in (0, 1))
BF16 = jnp.bfloat16
F32 = jnp.float32
VMEM = pl.BlockSpec(memory_space=pltpu.VMEM)
HBM = pl.BlockSpec(memory_space=pltpu.HBM)
SMEM = pl.BlockSpec(memory_space=pltpu.SMEM)
PARAMS = pltpu.CompilerParams(vmem_limit_bytes=24 * 1024 * 1024)


def swap_pairs(count, by, odd):
    pairs = []
    for low in range(count):
        if (low // by) % 2 == odd:
            high = (low + by) % count
            pairs += [(low, high), (high, low)]
    return pairs


def split3(value):
    high = value.astype(BF16)
    rest = value - high.astype(F32)
    mid = rest.astype(BF16)
    low = (rest - mid.astype(F32)).astype(BF16)
    return high, mid, low


def stacked(value, height):
    parts = split3(value)
    pad = jnp.zeros((height - 3, value.shape[1]), BF16)
    return jnp.concatenate([*parts, pad], axis=0)


def dot(a, b, dims, precision=None):
    return lax.dot_general(
        a, b, (dims, ((), ())), precision=precision, preferred_element_type=F32
    )


def is_low(place_ref, by):
    return lax.rem(lax.div(place_ref[0], by), 2) == 0


def turned(row):
    half = row.shape[1] // 2
    return jnp.concatenate([row[:, half:], row[:, :half]], axis=1)


def by_link(place_ref, row):
    parts = []
    for i, by in enumerate(FAR):
        pair = row[:, 2 * CAP * i : 2 * CAP * (i + 1)]
        parts.append(jnp.where(is_low(place_ref, by), pair, turned(pair)))
    return jnp.concatenate(parts, axis=1)


def as_rows(row):
    return jnp.concatenate([jnp.broadcast_to(row, (16, row.shape[1])).astype(BF16)] * (BLK // 16), axis=0)


def as_columns(row):
    return jnp.broadcast_to(row, (row.shape[1], row.shape[1])).T


def prepare_kernel(
    place_ref,
    dst_any,
    far_any,
    wts_any,
    cols_any,
    field_any,
    band_ref,
    hot_ref,
    coef_ref,
    field_ref,
    dst_ref,
    far_ref,
    wts_ref,
    cols_ref,
    sems,
):
    copies = [
        pltpu.make_async_copy(source, target, sems.at[i])
        for i, (source, target) in enumerate(
            (
                (dst_any, dst_ref),
                (far_any, far_ref),
                (wts_any, wts_ref),
                (cols_any, cols_ref),
                (field_any, field_ref),
            )
        )
    ]
    for copy in copies:
        copy.start()
    copies[0].wait()
    copies[1].wait()
    rows = cols_ref.shape[2]
    edges = dst_ref.shape[1]
    dst = by_link(place_ref, dst_ref[...])
    far = by_link(place_ref, far_ref[...])
    one, zero = jnp.ones((), BF16), jnp.zeros((), BF16)
    ids = lax.broadcasted_iota(jnp.int32, (BLK, edges), 0).astype(F32).astype(BF16)
    in_block = jnp.where(ids == as_rows(lax.rem(dst, BLK).astype(F32)), one, zero)
    owner = lax.div(dst, BLK)
    for b in range(rows // BLK):
        hot_ref[pl.ds(b * BLK, BLK), :] = in_block * as_rows(jnp.where(owner == b, 1.0, 0.0))
    hot = hot_ref[...]
    degree = jnp.sum(dot(stacked(far, 16), hot, ((1,), (1,))), axis=0, keepdims=True)
    copies[2].wait()
    for o in range(3):
        degree = degree + jnp.sum(wts_ref[o], axis=0, keepdims=True)
    at_edge = jnp.sum(dot(stacked(degree, 16), hot, ((1,), (0,))), axis=0, keepdims=True)
    far_coef = far / at_edge
    for i in range(edges // BLK):
        coef_ref[pl.ds(i * BLK, BLK), :] = as_columns(far_coef[:, i * BLK : (i + 1) * BLK])
    copies[3].wait()
    ids = ids[:, :BLK]
    for b in range(rows // BLK):
        block = pl.ds(b * BLK, BLK)
        degree_b = degree[:, b * BLK : (b + 1) * BLK]
        for o in range(3):
            cols = cols_ref[o, :, block].astype(F32)
            coef = wts_ref[o, :, block] / degree_b
            dense = jnp.zeros((BLK, BLK), BF16)
            for k in range(KB):
                here = ids == as_rows(cols[k : k + 1, :])
                dense = jnp.where(here, as_rows(coef[k : k + 1, :]), dense)
            band_ref[block, pl.ds(o * BLK, BLK)] = dense.T
    copies[4].wait()


def prepare(place, dst, far, wts, cols, field):
    rows, edges = cols.shape[2], dst.shape[1]
    return pl.pallas_call(
        prepare_kernel,
        out_shape=(
            jax.ShapeDtypeStruct((rows, 3 * BLK), BF16),
            jax.ShapeDtypeStruct((rows, edges), BF16),
            jax.ShapeDtypeStruct((edges, VECS), F32),
            jax.ShapeDtypeStruct(field.shape, BF16),
        ),
        in_specs=[SMEM, *(HBM,) * 5],
        out_specs=(VMEM,) * 4,
        scratch_shapes=[
            pltpu.VMEM(dst.shape, jnp.int32),
            pltpu.VMEM(far.shape, F32),
            pltpu.VMEM(wts.shape, F32),
            pltpu.VMEM(cols.shape, jnp.int32),
            pltpu.SemaphoreType.DMA((5,)),
        ],
        compiler_params=PARAMS,
        name="prepare",
    )(place, dst, far, wts, cols, field)


def send_out(even, first, last, picked, sent):
    sent = dict(zip(LINKS, sent, strict=True))
    sent[1, 0][...] = jnp.where(even, last, first)
    sent[1, 1][...] = jnp.where(even, first, last)
    for g, link in enumerate(FAR_LINKS):
        sent[link][:CAP, :] = picked[g * CAP : (g + 1) * CAP].astype(BF16)


def first_kernel(place_ref, field_ref, w0, w1, w2, w3, pick_mat_ref, *sent):
    rows = field_ref.shape[0]
    half = 2 * CAP
    lanes = lax.broadcasted_iota(jnp.int32, (1, half), 1)
    one, zero = jnp.ones((), BF16), jnp.zeros((), BF16)
    for i, (by, pair) in enumerate(zip(FAR, ((w0, w1), (w2, w3)), strict=True)):
        ahead, back = (w[:, i * half : (i + 1) * half] for w in pair)
        low = is_low(place_ref, by)
        ahead = jnp.where(low, turned(ahead), ahead)
        back = jnp.where(low, turned(back), back)
        wanted = jnp.where(lanes < CAP, ahead, back)
        column = as_columns(lax.rem(wanted, BLK).astype(F32)).astype(BF16)
        owner = as_columns(lax.div(wanted, BLK).astype(F32)).astype(BF16)
        ids = lax.broadcasted_iota(jnp.int32, (half, BLK), 1).astype(F32).astype(BF16)
        in_block = jnp.where(column == ids, one, zero)
        for b in range(rows // BLK):
            hot = jnp.where(owner == jnp.full((), b, BF16), in_block, zero)
            pick_mat_ref[pl.ds(i * half, half), pl.ds(b * BLK, BLK)] = hot
    field = field_ref[...]
    picked = dot(pick_mat_ref[...], field, ((1,), (0,)))
    send_out(is_low(place_ref, 1), field[:BLK], field[rows - BLK :], picked, sent)


SENT = tuple(jax.ShapeDtypeStruct((BLK, VECS), BF16) for _ in LINKS)


def first(place, field, wanted):
    rows = field.shape[0]
    return pl.pallas_call(
        first_kernel,
        out_shape=(jax.ShapeDtypeStruct((PEERS * CAP, rows), BF16), *SENT),
        in_specs=[SMEM] + [VMEM] * 5,
        out_specs=(VMEM,) * 7,
        compiler_params=PARAMS,
        name="first",
    )(place, field, *wanted)


def inner_kernel(scale, *refs):
    band_ref, field_ref, *prev_refs, part_ref = refs
    rows = field_ref.shape[0]
    count = rows // BLK
    for b in range(count):
        block = pl.ds(b * BLK, BLK)
        first, past = max(b - 1, 0), min(b + 2, count)
        value = scale * dot(
            band_ref[block, (first - b + 1) * BLK : (past - b + 1) * BLK],
            field_ref[first * BLK : past * BLK, :],
            ((1,), (0,)),
        )
        for prev_ref in prev_refs:
            value = value - prev_ref[block, :].astype(F32)
        part_ref[block, :] = value


def inner(scale, band, field, *prev):
    rows = field.shape[0]
    return pl.pallas_call(
        lambda *refs: inner_kernel(scale, *refs),
        out_shape=jax.ShapeDtypeStruct((rows, VECS), F32),
        in_specs=[VMEM] * (2 + len(prev)),
        out_specs=VMEM,
        compiler_params=PARAMS,
        cost_estimate=pl.CostEstimate(
            flops=2 * rows * 3 * BLK * VECS, bytes_accessed=4 * rows * 3 * BLK, transcendentals=0
        ),
        name="inner",
    )(band, field, *prev)


def advance(place_ref, band_ref, hot_ref, coef_ref, part_ref, got, scale, store):
    rows = part_ref.shape[0]
    count = rows // BLK
    even = is_low(place_ref, 1)
    got = dict(zip(LINKS, got, strict=True))
    low = jnp.where(even, got[1, 1][...], got[1, 0][...])
    high = jnp.where(even, got[1, 0][...], got[1, 1][...])
    far = jnp.concatenate([got[link][:CAP, :] for link in FAR_LINKS], axis=0)
    far = far.astype(F32) * coef_ref[...]
    far_high = far.astype(BF16)
    far_low = (far - far_high.astype(F32)).astype(BF16)
    far = jnp.concatenate([far_high, far_low], axis=1)
    for b in range(count):
        block = pl.ds(b * BLK, BLK)
        both = dot(hot_ref[block, :], far, ((1,), (0,)))
        total = both[:, :VECS] + both[:, VECS:]
        if b == 0:
            total += dot(band_ref[block, :BLK], low, ((1,), (0,)))
        if b == count - 1:
            total += dot(band_ref[block, 2 * BLK :], high, ((1,), (0,)))
        store(block, part_ref[block, :] + total * scale)
    return even


def step_kernel(scale, *refs):
    place_ref, band_ref, hot_ref, coef_ref, pick_mat_ref, part_ref = refs[:6]
    got, refs = refs[6:12], refs[12:]
    packed_ref, sent, next_refs = refs[0], refs[1:7], refs[7:]

    def store(block, value):
        for next_ref in next_refs:
            next_ref[block, :] = value
        packed_ref[block, :] = value.astype(BF16)

    even = advance(
        place_ref, band_ref, hot_ref, coef_ref, part_ref, got, scale, store
    )
    rows = part_ref.shape[0]
    picked = dot(pick_mat_ref[...], packed_ref[...], ((1,), (0,)))
    send_out(even, packed_ref[:BLK, :], packed_ref[rows - BLK :, :], picked, sent)


def step(scale, place, mats, part, got, has_next=True):
    rows = part.shape[0]
    return pl.pallas_call(
        lambda *refs: step_kernel(scale, *refs),
        out_shape=(
            jax.ShapeDtypeStruct((rows, VECS), BF16),
            *SENT,
            *(jax.ShapeDtypeStruct((rows, VECS), F32),) * has_next,
        ),
        in_specs=[SMEM] + [VMEM] * 11,
        out_specs=(VMEM,) * (7 + has_next),
        compiler_params=PARAMS,
        name="step",
    )(place, *mats, part, *got)


def last_kernel(scale, *refs):
    place_ref, band_ref, hot_ref, coef_ref, part_ref = refs[:5]
    got, (next_ref, kept_ref, sent_ref) = refs[5:11], refs[11:]

    def store(block, value):
        next_ref[block, :] = value

    advance(
        place_ref, band_ref, hot_ref, coef_ref, part_ref, got, scale, store
    )
    value = next_ref[...]
    gram = dot(value, value, ((0,), (0,)), lax.Precision.HIGHEST)
    half = VECS // 2
    low = is_low(place_ref, 1)
    kept_ref[...] = jnp.where(low, gram[:half], gram[half:])
    sent_ref[...] = jnp.where(low, gram[half:], gram[:half])


def last(scale, place, mats, part, got):
    rows = part.shape[0]
    return pl.pallas_call(
        lambda *refs: last_kernel(scale, *refs),
        out_shape=(
            jax.ShapeDtypeStruct((rows, VECS), F32),
            *(jax.ShapeDtypeStruct((VECS // 2, VECS), F32),) * 2,
        ),
        in_specs=[SMEM] + [VMEM] * 10,
        out_specs=(VMEM,) * 3,
        compiler_params=PARAMS,
        name="last",
    )(place, *mats, part, *got)


def total_of(terms):
    terms = list(terms)
    while len(terms) > 1:
        pairs = [terms[i] + terms[i + 1] for i in range(0, len(terms) - 1, 2)]
        terms = pairs + terms[len(terms) - len(terms) % 2 :]
    return terms[0]


def finish_kernel(scale, place_ref, own_ref, other_ref, field_ref, out_ref, inverse_ref):
    width = 8
    shape = (width, VECS)
    panels = VECS // width
    ids = lax.broadcasted_iota(jnp.int32, shape, 0)
    lanes = lax.broadcasted_iota(jnp.int32, shape, 1)

    def spread(value):
        return jnp.broadcast_to(value, shape)

    low = is_low(place_ref, 1)
    gram = jnp.concatenate(
        [
            jnp.where(low, own_ref[...], other_ref[...]),
            jnp.where(low, other_ref[...], own_ref[...]),
        ],
        axis=0,
    )
    left = [gram[width * b : width * (b + 1), :] for b in range(panels)]
    right = [jnp.where(ids + width * b == lanes, 1.0, 0.0) for b in range(panels)]
    for p in range(panels):
        base = width * p
        columns = [spread(left[p][:, base + c : base + c + 1]) for c in range(width)]
        entry = {
            (i, c): spread(columns[c][i : i + 1, :]) for i in range(width) for c in range(i + 1)
        }
        inverse, l, n = [], {}, {}
        for j in range(width):
            inverse.append(1.0 / entry[j, j])
            for i in range(j + 1, width):
                l[i, j] = entry[i, j] * inverse[j]
            for c in range(j + 1, width):
                for i in range(c, width):
                    entry[i, c] = entry[i, c] - l[i, j] * entry[c, j]
        for j in range(width):
            for i in range(j + 1, width):
                n[i, j] = -total_of([l[i, j], *(l[i, m] * n[m, j] for m in range(j + 1, i))])
        factors = []
        for side in (left, right):
            raw = [spread(side[p][i : i + 1, :]) for i in range(width)]
            done = [total_of([raw[i], *(n[i, j] * raw[j] for j in range(i))]) for i in range(width)]
            if side is right:
                for i in range(width):
                    row = done[i] * (lax.rsqrt(entry[i, i]) * scale)
                    inverse_ref[base + i : base + i + 1, :] = row[:1, :]
            done = [d * v for d, v in zip(done, inverse)]
            factors.append(
                [
                    total_of([done[c], *(n[i, c] * done[i] for i in range(c + 1, width))])
                    for c in range(width)
                ]
            )
        for b in range(p + 1, panels):
            columns = [spread(left[b][:, base + c : base + c + 1]) for c in range(width)]
            for side, rows in zip((left, right), factors):
                side[b] = side[b] - total_of(c * r for c, r in zip(columns, rows))
    out_ref[...] = dot(field_ref[...], inverse_ref[...], ((1,), (1,)), lax.Precision.HIGHEST)


def finish(scale, place, halves, field):
    return pl.pallas_call(
        lambda *refs: finish_kernel(scale, *refs),
        out_shape=jax.ShapeDtypeStruct(field.shape, F32),
        in_specs=[SMEM] + [VMEM] * 3,
        out_specs=VMEM,
        scratch_shapes=[pltpu.VMEM((VECS, VECS), F32)],
        compiler_params=PARAMS,
        name="finish",
    )(place, *halves, field)


def summed(kept, sent, count):
    def swapped(value, mask):
        return lax.ppermute(value, AXES, [(i, i ^ mask) for i in range(count)])

    bits = [1 << i for i in range(1, count.bit_length() - 1)]
    half = kept + swapped(sent, 1)
    for i in range(0, len(bits), 2):
        stage = bits[i : i + 2]
        masks = stage if len(stage) == 1 else [*stage, stage[0] ^ stage[1]]
        half = sum((swapped(half, mask) for mask in masks), half)
    return half, swapped(half, 1)


def local(start_basis, band_cols, band_wts, far_dst, far_src, far_wts):
    count = lax.axis_size(AXES)
    place = lax.axis_index(AXES)
    total_rows = start_basis.shape[0] * count

    def swap(value, by, odd):
        return lax.ppermute(value, AXES, swap_pairs(count, by, odd))

    def as_row(value):
        return value.reshape(1, -1)

    asked = as_row(far_src)
    wanted = [swap(asked, *link) for link in FAR_LINKS]
    here = place.astype(jnp.int32).reshape(1)
    band, hot, coef, field = prepare(
        here,
        *(
            pltpu.with_memory_space_constraint(v, pltpu.HBM)
            for v in (
                as_row(far_dst),
                as_row(far_wts),
                jnp.transpose(band_wts, (1, 2, 0)),
                jnp.transpose(band_cols, (1, 2, 0)),
                start_basis,
            )
        ),
    )
    wanted, band = lax.optimization_barrier((wanted, band))
    pick_mat, *sent = first(here, field, wanted)

    def exchange(sent):
        return [swap(v, *link) for v, link in zip(sent, LINKS, strict=True)]

    mats = (band, hot, coef, pick_mat)
    previous, packed = (), field
    for k in range(DEGREE):
        scale = (2.0 if k else 1.0) / HALF_WIDTH
        got = exchange(sent)
        part = inner(scale, band, packed, *previous)
        if k == DEGREE - 1:
            filtered, kept, sent = last(scale, here, mats[:3], part, got)
        else:
            previous = (current,) if k else (field,)
            has_next = k < DEGREE - 2
            packed, *sent = step(scale, here, mats, part, got, has_next)
            if has_next:
                current = sent.pop()
    return finish(math.sqrt(total_rows), here, summed(kept, sent, count), filtered)


def solution(mesh):
    placed = (
        P(AXES, None),
        P(AXES, None, None),
        P(AXES, None, None),
        P(AXES),
        P(AXES),
        P(AXES),
    )
    return jax.shard_map(
        local, mesh=mesh, in_specs=placed, out_specs=P(AXES, None), check_vma=False
    )
```

```python
import math

import jax
import jax.numpy as jnp
from jax import lax
from jax.experimental import pallas as pl
from jax.experimental.pallas import tpu as pltpu
from jax.sharding import PartitionSpec as P

VECS = 128
BLK = 128
KB = 8
PEERS = 4
CAP = 64
DEGREE = 8
HALF_WIDTH = 0.95
AXES = ("row", "snk")
FAR = (2, 4)
LINKS = ((4, 1), (2, 1), (1, 1), (4, 0), (2, 0), (1, 0))
FAR_LINKS = tuple((by, odd) for by in FAR for odd in (0, 1))
BF16 = jnp.bfloat16
F32 = jnp.float32
VMEM = pl.BlockSpec(memory_space=pltpu.VMEM)
HBM = pl.BlockSpec(memory_space=pltpu.HBM)
SMEM = pl.BlockSpec(memory_space=pltpu.SMEM)
PARAMS = pltpu.CompilerParams(vmem_limit_bytes=24 * 1024 * 1024)


def swap_pairs(count, by, odd):
    pairs = []
    for low in range(count):
        if (low // by) % 2 == odd:
            high = (low + by) % count
            pairs += [(low, high), (high, low)]
    return pairs


def split3(value):
    high = value.astype(BF16)
    rest = value - high.astype(F32)
    mid = rest.astype(BF16)
    low = (rest - mid.astype(F32)).astype(BF16)
    return high, mid, low


def stacked(value, height):
    parts = split3(value)
    pad = jnp.zeros((height - 3, value.shape[1]), BF16)
    return jnp.concatenate([*parts, pad], axis=0)


def dot(a, b, dims, precision=None):
    return lax.dot_general(
        a, b, (dims, ((), ())), precision=precision, preferred_element_type=F32
    )


def is_low(place_ref, by):
    return lax.rem(lax.div(place_ref[0], by), 2) == 0


def turned(row):
    half = row.shape[1] // 2
    return jnp.concatenate([row[:, half:], row[:, :half]], axis=1)


def by_link(place_ref, row):
    parts = []
    for i, by in enumerate(FAR):
        pair = row[:, 2 * CAP * i : 2 * CAP * (i + 1)]
        parts.append(jnp.where(is_low(place_ref, by), pair, turned(pair)))
    return jnp.concatenate(parts, axis=1)


def as_rows(row):
    return jnp.concatenate([jnp.broadcast_to(row, (16, row.shape[1])).astype(BF16)] * (BLK // 16), axis=0)


def as_columns(row):
    return jnp.broadcast_to(row, (row.shape[1], row.shape[1])).T


def prepare_kernel(
    place_ref,
    dst_any,
    far_any,
    wts_any,
    cols_any,
    field_any,
    band_ref,
    hot_ref,
    coef_ref,
    field_ref,
    dst_ref,
    far_ref,
    wts_ref,
    cols_ref,
    sems,
):
    copies = [
        pltpu.make_async_copy(source, target, sems.at[i])
        for i, (source, target) in enumerate(
            (
                (dst_any, dst_ref),
                (far_any, far_ref),
                (wts_any, wts_ref),
                (cols_any, cols_ref),
                (field_any, field_ref),
            )
        )
    ]
    for copy in copies:
        copy.start()
    copies[0].wait()
    copies[1].wait()
    rows = cols_ref.shape[2]
    edges = dst_ref.shape[1]
    dst = by_link(place_ref, dst_ref[...])
    far = by_link(place_ref, far_ref[...])
    one, zero = jnp.ones((), BF16), jnp.zeros((), BF16)
    ids = lax.broadcasted_iota(jnp.int32, (BLK, edges), 0).astype(F32).astype(BF16)
    in_block = jnp.where(ids == as_rows(lax.rem(dst, BLK).astype(F32)), one, zero)
    owner = lax.div(dst, BLK)
    for b in range(rows // BLK):
        hot_ref[pl.ds(b * BLK, BLK), :] = in_block * as_rows(jnp.where(owner == b, 1.0, 0.0))
    hot = hot_ref[...]
    degree = jnp.sum(dot(stacked(far, 16), hot, ((1,), (1,))), axis=0, keepdims=True)
    copies[2].wait()
    for o in range(3):
        degree = degree + jnp.sum(wts_ref[o], axis=0, keepdims=True)
    at_edge = jnp.sum(dot(stacked(degree, 16), hot, ((1,), (0,))), axis=0, keepdims=True)
    far_coef = far / at_edge
    for i in range(edges // BLK):
        coef_ref[pl.ds(i * BLK, BLK), :] = as_columns(far_coef[:, i * BLK : (i + 1) * BLK])
    copies[3].wait()
    ids = ids[:, :BLK]
    for b in range(rows // BLK):
        block = pl.ds(b * BLK, BLK)
        degree_b = degree[:, b * BLK : (b + 1) * BLK]
        for o in range(3):
            cols = cols_ref[o, :, block].astype(F32)
            coef = wts_ref[o, :, block] / degree_b
            dense = jnp.zeros((BLK, BLK), BF16)
            for k in range(KB):
                here = ids == as_rows(cols[k : k + 1, :])
                dense = jnp.where(here, as_rows(coef[k : k + 1, :]), dense)
            band_ref[block, pl.ds(o * BLK, BLK)] = dense.T
    copies[4].wait()


def prepare(place, dst, far, wts, cols, field):
    rows, edges = cols.shape[2], dst.shape[1]
    return pl.pallas_call(
        prepare_kernel,
        out_shape=(
            jax.ShapeDtypeStruct((rows, 3 * BLK), BF16),
            jax.ShapeDtypeStruct((rows, edges), BF16),
            jax.ShapeDtypeStruct((edges, VECS), F32),
            jax.ShapeDtypeStruct(field.shape, BF16),
        ),
        in_specs=[SMEM, *(HBM,) * 5],
        out_specs=(VMEM,) * 4,
        scratch_shapes=[
            pltpu.VMEM(dst.shape, jnp.int32),
            pltpu.VMEM(far.shape, F32),
            pltpu.VMEM(wts.shape, F32),
            pltpu.VMEM(cols.shape, jnp.int32),
            pltpu.SemaphoreType.DMA((5,)),
        ],
        compiler_params=PARAMS,
        name="prepare",
    )(place, dst, far, wts, cols, field)


def send_out(even, first, last, picked, sent):
    sent = dict(zip(LINKS, sent, strict=True))
    sent[1, 0][...] = jnp.where(even, last, first)
    sent[1, 1][...] = jnp.where(even, first, last)
    for g, link in enumerate(FAR_LINKS):
        sent[link][:CAP, :] = picked[g * CAP : (g + 1) * CAP].astype(BF16)


def first_kernel(place_ref, field_ref, w0, w1, w2, w3, pick_mat_ref, *sent):
    rows = field_ref.shape[0]
    half = 2 * CAP
    lanes = lax.broadcasted_iota(jnp.int32, (1, half), 1)
    one, zero = jnp.ones((), BF16), jnp.zeros((), BF16)
    for i, (by, pair) in enumerate(zip(FAR, ((w0, w1), (w2, w3)), strict=True)):
        ahead, back = (w[:, i * half : (i + 1) * half] for w in pair)
        low = is_low(place_ref, by)
        ahead = jnp.where(low, turned(ahead), ahead)
        back = jnp.where(low, turned(back), back)
        wanted = jnp.where(lanes < CAP, ahead, back)
        column = as_columns(lax.rem(wanted, BLK).astype(F32)).astype(BF16)
        owner = as_columns(lax.div(wanted, BLK).astype(F32)).astype(BF16)
        ids = lax.broadcasted_iota(jnp.int32, (half, BLK), 1).astype(F32).astype(BF16)
        in_block = jnp.where(column == ids, one, zero)
        for b in range(rows // BLK):
            hot = jnp.where(owner == jnp.full((), b, BF16), in_block, zero)
            pick_mat_ref[pl.ds(i * half, half), pl.ds(b * BLK, BLK)] = hot
    field = field_ref[...]
    picked = dot(pick_mat_ref[...], field, ((1,), (0,)))
    send_out(is_low(place_ref, 1), field[:BLK], field[rows - BLK :], picked, sent)


SENT = tuple(jax.ShapeDtypeStruct((BLK, VECS), BF16) for _ in LINKS)


def first(place, field, wanted):
    rows = field.shape[0]
    return pl.pallas_call(
        first_kernel,
        out_shape=(jax.ShapeDtypeStruct((PEERS * CAP, rows), BF16), *SENT),
        in_specs=[SMEM] + [VMEM] * 5,
        out_specs=(VMEM,) * 7,
        compiler_params=PARAMS,
        name="first",
    )(place, field, *wanted)


def with_parts(value):
    high = value.astype(BF16)
    low = (value - high.astype(F32)).astype(BF16)
    return jnp.concatenate([high, low], axis=1)


def parts_joined(both):
    half = both.shape[1] // 2
    return both[:, :half] + both[:, half:]


def far_parts(coef_ref, got):
    far = jnp.concatenate([got[link][:CAP, :] for link in FAR_LINKS], axis=0)
    return with_parts(far.astype(F32) * coef_ref[...])


def inner_walk(scale, band_ref, field_ref, prev_refs, part_ref):
    rows = field_ref.shape[0]
    count = rows // BLK
    for b in range(count):
        block = pl.ds(b * BLK, BLK)
        first, past = max(b - 1, 0), min(b + 2, count)
        value = scale * dot(
            band_ref[block, (first - b + 1) * BLK : (past - b + 1) * BLK],
            field_ref[first * BLK : past * BLK, :],
            ((1,), (0,)),
        )
        for prev_ref in prev_refs:
            value = value - prev_ref[block, :].astype(F32)
        part_ref[block, :] = value


def inside_of(ref):
    return slice(BLK, ref.shape[0] - BLK)


def picked_parts(pick_mat_ref, part_ref):
    inside = inside_of(part_ref)
    both = dot(pick_mat_ref[:, inside], with_parts(part_ref[inside, :]), ((1,), (0,)))
    return parts_joined(both)


def opening_kernel(scale, band_ref, hot_ref, pick_mat_ref, field_ref, part_ref, picked_ref, joint_ref):
    inner_walk(scale, band_ref, field_ref, (), part_ref)
    picked_ref[...] = picked_parts(pick_mat_ref, part_ref)
    inside = inside_of(hot_ref)
    joint = dot(pick_mat_ref[:, inside], hot_ref[inside, :], ((1,), (0,)))
    joint_ref[...] = joint.astype(BF16)


def opening(scale, band, hot, pick_mat, field):
    rows, edges = hot.shape
    return pl.pallas_call(
        lambda *refs: opening_kernel(scale, *refs),
        out_shape=(
            jax.ShapeDtypeStruct((rows, VECS), F32),
            jax.ShapeDtypeStruct((edges, VECS), F32),
            jax.ShapeDtypeStruct((edges, edges), BF16),
        ),
        in_specs=[VMEM] * 4,
        out_specs=(VMEM,) * 3,
        compiler_params=PARAMS,
        cost_estimate=estimate(rows),
        name="opening",
    )(band, hot, pick_mat, field)


def estimate(rows):
    return pl.CostEstimate(
        flops=2 * rows * 3 * BLK * VECS, bytes_accessed=4 * rows * 3 * BLK, transcendentals=0
    )


def inner_kernel(scale, before_scale, more, *refs):
    band_ref, hot_ref, pick_mat_ref, known_ref, far_ref, edge_ref, prev_ref = refs[:7]
    part_ref, more_refs, packed_ref = refs[7], refs[8:-1], refs[-1]
    rows = known_ref.shape[0]
    count = rows // BLK
    for b in range(count):
        block = pl.ds(b * BLK, BLK)
        if b == 0:
            value = edge_ref[:BLK, :]
        elif b == count - 1:
            value = edge_ref[BLK:, :]
        else:
            both = dot(hot_ref[block, :], far_ref[...], ((1,), (0,)))
            value = known_ref[block, :] + parts_joined(both) * before_scale
        if more:
            more_refs[0][block, :] = value
        packed_ref[block, :] = value.astype(BF16)
    inner_walk(scale, band_ref, packed_ref, (prev_ref,), part_ref)
    if more:
        more_refs[1][...] = picked_parts(pick_mat_ref, part_ref)


def inner(scale, before_scale, more, band, hot, pick_mat, known, far, edge, prev):
    rows, edges = hot.shape
    return pl.pallas_call(
        lambda *refs: inner_kernel(scale, before_scale, more, *refs),
        out_shape=(
            jax.ShapeDtypeStruct((rows, VECS), F32),
            *(
                jax.ShapeDtypeStruct((rows, VECS), F32),
                jax.ShapeDtypeStruct((edges, VECS), F32),
            )[: 2 * more],
        ),
        in_specs=[VMEM] * 7,
        out_specs=(VMEM,) * (1 + 2 * more),
        scratch_shapes=[pltpu.VMEM((rows, VECS), BF16)],
        compiler_params=PARAMS,
        cost_estimate=estimate(rows),
        name="inner",
    )(band, hot, pick_mat, known, far, edge, prev)


def advance(place_ref, band_ref, hot_ref, coef_ref, part_ref, got, scale, store, blocks):
    rows = part_ref.shape[0]
    count = rows // BLK
    even = is_low(place_ref, 1)
    got = dict(zip(LINKS, got, strict=True))
    low = jnp.where(even, got[1, 1][...], got[1, 0][...])
    high = jnp.where(even, got[1, 0][...], got[1, 1][...])
    far = far_parts(coef_ref, got)
    for b in blocks:
        block = pl.ds(b * BLK, BLK)
        total = parts_joined(dot(hot_ref[block, :], far, ((1,), (0,))))
        if b == 0:
            total += dot(band_ref[block, :BLK], low, ((1,), (0,)))
        if b == count - 1:
            total += dot(band_ref[block, 2 * BLK :], high, ((1,), (0,)))
        store(block, part_ref[block, :] + total * scale)
    return even, far


def step_kernel(scale, *refs):
    place_ref, band_ref, hot_ref, coef_ref, joint_ref, pick_mat_ref, part_ref, picked_ref = refs[:8]
    got, sent, (far_ref, edge_ref) = refs[8:14], refs[14:20], refs[20:]
    rows = part_ref.shape[0]
    ends = []

    def store(block, value):
        edge_ref[pl.ds(len(ends) * BLK, BLK), :] = value
        ends.append(value.astype(BF16))

    even, far = advance(
        place_ref,
        band_ref,
        hot_ref,
        coef_ref,
        part_ref,
        got,
        scale,
        store,
        (0, rows // BLK - 1),
    )
    far_ref[...] = far
    first, last = ends
    picked = picked_ref[...] + parts_joined(dot(joint_ref[...], far, ((1,), (0,)))) * scale
    picked += dot(pick_mat_ref[:, :BLK], first, ((1,), (0,)))
    picked += dot(pick_mat_ref[:, rows - BLK :], last, ((1,), (0,)))
    send_out(even, first, last, picked, sent)


def step(scale, place, mats, part, picked, got):
    edges = picked.shape[0]
    *sent, far, edge = pl.pallas_call(
        lambda *refs: step_kernel(scale, *refs),
        out_shape=(
            *SENT,
            jax.ShapeDtypeStruct((edges, 2 * VECS), BF16),
            jax.ShapeDtypeStruct((2 * BLK, VECS), F32),
        ),
        in_specs=[SMEM] + [VMEM] * 13,
        out_specs=(VMEM,) * 8,
        compiler_params=PARAMS,
        name="step",
    )(place, *mats, part, picked, *got)
    return sent, far, edge


def last_kernel(scale, *refs):
    place_ref, band_ref, hot_ref, coef_ref, part_ref = refs[:5]
    got, (next_ref, kept_ref, sent_ref) = refs[5:11], refs[11:]

    def store(block, value):
        next_ref[block, :] = value

    advance(
        place_ref,
        band_ref,
        hot_ref,
        coef_ref,
        part_ref,
        got,
        scale,
        store,
        range(part_ref.shape[0] // BLK),
    )
    value = next_ref[...]
    gram = dot(value, value, ((0,), (0,)), lax.Precision.HIGHEST)
    half = VECS // 2
    low = is_low(place_ref, 1)
    kept_ref[...] = jnp.where(low, gram[:half], gram[half:])
    sent_ref[...] = jnp.where(low, gram[half:], gram[:half])


def last(scale, place, mats, part, got):
    rows = part.shape[0]
    return pl.pallas_call(
        lambda *refs: last_kernel(scale, *refs),
        out_shape=(
            jax.ShapeDtypeStruct((rows, VECS), F32),
            *(jax.ShapeDtypeStruct((VECS // 2, VECS), F32),) * 2,
        ),
        in_specs=[SMEM] + [VMEM] * 10,
        out_specs=(VMEM,) * 3,
        compiler_params=PARAMS,
        name="last",
    )(place, *mats, part, *got)


def total_of(terms):
    terms = list(terms)
    while len(terms) > 1:
        pairs = [terms[i] + terms[i + 1] for i in range(0, len(terms) - 1, 2)]
        terms = pairs + terms[len(terms) - len(terms) % 2 :]
    return terms[0]


def finish_kernel(scale, place_ref, own_ref, other_ref, field_ref, out_ref, inverse_ref):
    width = 8
    shape = (width, VECS)
    panels = VECS // width
    ids = lax.broadcasted_iota(jnp.int32, shape, 0)
    lanes = lax.broadcasted_iota(jnp.int32, shape, 1)

    def spread(value):
        return jnp.broadcast_to(value, shape)

    low = is_low(place_ref, 1)
    gram = jnp.concatenate(
        [
            jnp.where(low, own_ref[...], other_ref[...]),
            jnp.where(low, other_ref[...], own_ref[...]),
        ],
        axis=0,
    )
    left = [gram[width * b : width * (b + 1), :] for b in range(panels)]
    right = [jnp.where(ids + width * b == lanes, 1.0, 0.0) for b in range(panels)]
    for p in range(panels):
        base = width * p
        columns = [spread(left[p][:, base + c : base + c + 1]) for c in range(width)]
        entry = {
            (i, c): spread(columns[c][i : i + 1, :]) for i in range(width) for c in range(i + 1)
        }
        inverse, l, n = [], {}, {}
        for j in range(width):
            inverse.append(1.0 / entry[j, j])
            for i in range(j + 1, width):
                l[i, j] = entry[i, j] * inverse[j]
            for c in range(j + 1, width):
                for i in range(c, width):
                    entry[i, c] = entry[i, c] - l[i, j] * entry[c, j]
        for j in range(width):
            for i in range(j + 1, width):
                n[i, j] = -total_of([l[i, j], *(l[i, m] * n[m, j] for m in range(j + 1, i))])
        factors = []
        for side in (left, right):
            raw = [spread(side[p][i : i + 1, :]) for i in range(width)]
            done = [total_of([raw[i], *(n[i, j] * raw[j] for j in range(i))]) for i in range(width)]
            if side is right:
                for i in range(width):
                    row = done[i] * (lax.rsqrt(entry[i, i]) * scale)
                    inverse_ref[base + i : base + i + 1, :] = row[:1, :]
            done = [d * v for d, v in zip(done, inverse)]
            factors.append(
                [
                    total_of([done[c], *(n[i, c] * done[i] for i in range(c + 1, width))])
                    for c in range(width)
                ]
            )
        for b in range(p + 1, panels):
            columns = [spread(left[b][:, base + c : base + c + 1]) for c in range(width)]
            for side, rows in zip((left, right), factors):
                side[b] = side[b] - total_of(c * r for c, r in zip(columns, rows))
    out_ref[...] = dot(field_ref[...], inverse_ref[...], ((1,), (1,)), lax.Precision.HIGHEST)


def finish(scale, place, halves, field):
    return pl.pallas_call(
        lambda *refs: finish_kernel(scale, *refs),
        out_shape=jax.ShapeDtypeStruct(field.shape, F32),
        in_specs=[SMEM] + [VMEM] * 3,
        out_specs=VMEM,
        scratch_shapes=[pltpu.VMEM((VECS, VECS), F32)],
        compiler_params=PARAMS,
        name="finish",
    )(place, *halves, field)


def summed(kept, sent, count):
    def swapped(value, mask):
        return lax.ppermute(value, AXES, [(i, i ^ mask) for i in range(count)])

    bits = [1 << i for i in range(1, count.bit_length() - 1)]
    half = kept + swapped(sent, 1)
    for i in range(0, len(bits), 2):
        stage = bits[i : i + 2]
        masks = stage if len(stage) == 1 else [*stage, stage[0] ^ stage[1]]
        half = sum((swapped(half, mask) for mask in masks), half)
    return half, swapped(half, 1)


def local(start_basis, band_cols, band_wts, far_dst, far_src, far_wts):
    count = lax.axis_size(AXES)
    place = lax.axis_index(AXES)
    total_rows = start_basis.shape[0] * count

    def swap(value, by, odd):
        return lax.ppermute(value, AXES, swap_pairs(count, by, odd))

    def as_row(value):
        return value.reshape(1, -1)

    asked = as_row(far_src)
    wanted = [swap(asked, *link) for link in FAR_LINKS]
    here = place.astype(jnp.int32).reshape(1)
    band, hot, coef, field = prepare(
        here,
        *(
            pltpu.with_memory_space_constraint(v, pltpu.HBM)
            for v in (
                as_row(far_dst),
                as_row(far_wts),
                jnp.transpose(band_wts, (1, 2, 0)),
                jnp.transpose(band_cols, (1, 2, 0)),
                start_basis,
            )
        ),
    )
    wanted, band = lax.optimization_barrier((wanted, band))
    pick_mat, *sent = first(here, field, wanted)

    def exchange(sent):
        return [swap(v, *link) for v, link in zip(sent, LINKS, strict=True)]

    got = exchange(sent)
    before, scale = 1.0 / HALF_WIDTH, 2.0 / HALF_WIDTH
    part, picked, joint = opening(before, band, hot, pick_mat, field)
    previous = field
    for k in range(1, DEGREE):
        mats = (band, hot, coef, joint, pick_mat)
        sent, far, edge = step(before, here, mats, part, picked, got)
        got = exchange(sent)
        more = k < DEGREE - 1
        part, *rest = inner(scale, before, more, band, hot, pick_mat, part, far, edge, previous)
        if more:
            previous, picked = rest
        before = scale
    filtered, kept, sent = last(scale, here, (band, hot, coef), part, got)
    return finish(math.sqrt(total_rows), here, summed(kept, sent, count), filtered)


def solution(mesh):
    placed = (
        P(AXES, None),
        P(AXES, None, None),
        P(AXES, None, None),
        P(AXES),
        P(AXES),
        P(AXES),
    )
    return jax.shard_map(
        local, mesh=mesh, in_specs=placed, out_specs=P(AXES, None), check_vma=False
    )
```

```python
import math

import jax
import jax.numpy as jnp
from jax import lax
from jax.experimental import pallas as pl
from jax.experimental.pallas import tpu as pltpu
from jax.sharding import PartitionSpec as P

VECS = 128
BLK = 128
KB = 8
PEERS = 4
CAP = 64
DEGREE = 8
HALF_WIDTH = 0.95
AXES = ("row", "snk")
FAR = (2, 4)
LINKS = ((4, 1), (2, 1), (1, 1), (4, 0), (2, 0), (1, 0))
FAR_LINKS = tuple((by, odd) for by in FAR for odd in (0, 1))
BF16 = jnp.bfloat16
F32 = jnp.float32
VMEM = pl.BlockSpec(memory_space=pltpu.VMEM)
HBM = pl.BlockSpec(memory_space=pltpu.HBM)
SMEM = pl.BlockSpec(memory_space=pltpu.SMEM)
PARAMS = pltpu.CompilerParams(vmem_limit_bytes=24 * 1024 * 1024)


def swap_pairs(count, by, odd):
    pairs = []
    for low in range(count):
        if (low // by) % 2 == odd:
            high = (low + by) % count
            pairs += [(low, high), (high, low)]
    return pairs


def split3(value):
    high = value.astype(BF16)
    rest = value - high.astype(F32)
    mid = rest.astype(BF16)
    low = (rest - mid.astype(F32)).astype(BF16)
    return high, mid, low


def stacked(value, height):
    parts = split3(value)
    pad = jnp.zeros((height - 3, value.shape[1]), BF16)
    return jnp.concatenate([*parts, pad], axis=0)


def dot(a, b, dims, precision=None):
    return lax.dot_general(
        a, b, (dims, ((), ())), precision=precision, preferred_element_type=F32
    )


def is_low(place_ref, by):
    return lax.rem(lax.div(place_ref[0], by), 2) == 0


def turned(row):
    half = row.shape[1] // 2
    return jnp.concatenate([row[:, half:], row[:, :half]], axis=1)


def by_link(place_ref, row):
    parts = []
    for i, by in enumerate(FAR):
        pair = row[:, 2 * CAP * i : 2 * CAP * (i + 1)]
        parts.append(jnp.where(is_low(place_ref, by), pair, turned(pair)))
    return jnp.concatenate(parts, axis=1)


def as_rows(row):
    return jnp.concatenate([jnp.broadcast_to(row, (16, row.shape[1])).astype(BF16)] * (BLK // 16), axis=0)


def as_columns(row):
    return jnp.broadcast_to(row, (row.shape[1], row.shape[1])).T


def prepare_kernel(
    place_ref,
    dst_any,
    far_any,
    wts_any,
    cols_any,
    field_any,
    band_ref,
    hot_ref,
    coef_ref,
    field_ref,
    dst_ref,
    far_ref,
    wts_ref,
    cols_ref,
    sems,
):
    copies = [
        pltpu.make_async_copy(source, target, sems.at[i])
        for i, (source, target) in enumerate(
            (
                (dst_any, dst_ref),
                (far_any, far_ref),
                (wts_any, wts_ref),
                (cols_any, cols_ref),
                (field_any, field_ref),
            )
        )
    ]
    for copy in copies:
        copy.start()
    copies[0].wait()
    copies[1].wait()
    rows = cols_ref.shape[2]
    edges = dst_ref.shape[1]
    dst = by_link(place_ref, dst_ref[...])
    far = by_link(place_ref, far_ref[...])
    one, zero = jnp.ones((), BF16), jnp.zeros((), BF16)
    ids = lax.broadcasted_iota(jnp.int32, (BLK, edges), 0).astype(F32).astype(BF16)
    in_block = jnp.where(ids == as_rows(lax.rem(dst, BLK).astype(F32)), one, zero)
    owner = lax.div(dst, BLK)
    for b in range(rows // BLK):
        hot_ref[pl.ds(b * BLK, BLK), :] = in_block * as_rows(jnp.where(owner == b, 1.0, 0.0))
    hot = hot_ref[...]
    degree = jnp.sum(dot(stacked(far, 16), hot, ((1,), (1,))), axis=0, keepdims=True)
    copies[2].wait()
    for o in range(3):
        degree = degree + jnp.sum(wts_ref[o], axis=0, keepdims=True)
    at_edge = jnp.sum(dot(stacked(degree, 16), hot, ((1,), (0,))), axis=0, keepdims=True)
    far_coef = far / at_edge
    for i in range(edges // BLK):
        coef_ref[pl.ds(i * BLK, BLK), :] = as_columns(far_coef[:, i * BLK : (i + 1) * BLK])
    copies[3].wait()
    ids = ids[:, :BLK]
    for b in range(rows // BLK):
        block = pl.ds(b * BLK, BLK)
        degree_b = degree[:, b * BLK : (b + 1) * BLK]
        for o in range(3):
            cols = cols_ref[o, :, block].astype(F32)
            coef = wts_ref[o, :, block] / degree_b
            dense = jnp.zeros((BLK, BLK), BF16)
            for k in range(KB):
                here = ids == as_rows(cols[k : k + 1, :])
                dense = jnp.where(here, as_rows(coef[k : k + 1, :]), dense)
            band_ref[block, pl.ds(o * BLK, BLK)] = dense.T
    copies[4].wait()


def prepare(place, dst, far, wts, cols, field):
    rows, edges = cols.shape[2], dst.shape[1]
    return pl.pallas_call(
        prepare_kernel,
        out_shape=(
            jax.ShapeDtypeStruct((rows, 3 * BLK), BF16),
            jax.ShapeDtypeStruct((rows, edges), BF16),
            jax.ShapeDtypeStruct((edges, VECS), F32),
            jax.ShapeDtypeStruct(field.shape, BF16),
        ),
        in_specs=[SMEM, *(HBM,) * 5],
        out_specs=(VMEM,) * 4,
        scratch_shapes=[
            pltpu.VMEM(dst.shape, jnp.int32),
            pltpu.VMEM(far.shape, F32),
            pltpu.VMEM(wts.shape, F32),
            pltpu.VMEM(cols.shape, jnp.int32),
            pltpu.SemaphoreType.DMA((5,)),
        ],
        compiler_params=PARAMS,
        name="prepare",
    )(place, dst, far, wts, cols, field)


def send_out(even, first, last, picked, sent):
    sent = dict(zip(LINKS, sent, strict=True))
    sent[1, 0][...] = jnp.where(even, last, first)
    sent[1, 1][...] = jnp.where(even, first, last)
    for g, link in enumerate(FAR_LINKS):
        sent[link][:CAP, :] = picked[g * CAP : (g + 1) * CAP].astype(BF16)


def first_kernel(place_ref, field_ref, w0, w1, w2, w3, pick_mat_ref, *sent):
    rows = field_ref.shape[0]
    half = 2 * CAP
    lanes = lax.broadcasted_iota(jnp.int32, (1, half), 1)
    one, zero = jnp.ones((), BF16), jnp.zeros((), BF16)
    for i, (by, pair) in enumerate(zip(FAR, ((w0, w1), (w2, w3)), strict=True)):
        ahead, back = (w[:, i * half : (i + 1) * half] for w in pair)
        low = is_low(place_ref, by)
        ahead = jnp.where(low, turned(ahead), ahead)
        back = jnp.where(low, turned(back), back)
        wanted = jnp.where(lanes < CAP, ahead, back)
        column = as_columns(lax.rem(wanted, BLK).astype(F32)).astype(BF16)
        owner = as_columns(lax.div(wanted, BLK).astype(F32)).astype(BF16)
        ids = lax.broadcasted_iota(jnp.int32, (half, BLK), 1).astype(F32).astype(BF16)
        in_block = jnp.where(column == ids, one, zero)
        for b in range(rows // BLK):
            hot = jnp.where(owner == jnp.full((), b, BF16), in_block, zero)
            pick_mat_ref[pl.ds(i * half, half), pl.ds(b * BLK, BLK)] = hot
    field = field_ref[...]
    picked = dot(pick_mat_ref[...], field, ((1,), (0,)))
    send_out(is_low(place_ref, 1), field[:BLK], field[rows - BLK :], picked, sent)


SENT = tuple(jax.ShapeDtypeStruct((BLK, VECS), BF16) for _ in LINKS)


def first(place, field, wanted):
    rows = field.shape[0]
    return pl.pallas_call(
        first_kernel,
        out_shape=(jax.ShapeDtypeStruct((PEERS * CAP, rows), BF16), *SENT),
        in_specs=[SMEM] + [VMEM] * 5,
        out_specs=(VMEM,) * 7,
        compiler_params=PARAMS,
        name="first",
    )(place, field, *wanted)


def with_parts(value):
    high = value.astype(BF16)
    low = (value - high.astype(F32)).astype(BF16)
    return jnp.concatenate([high, low], axis=1)


def parts_joined(both):
    half = both.shape[1] // 2
    return both[:, :half] + both[:, half:]


def far_parts(coef_ref, got):
    far = jnp.concatenate([got[link][:CAP, :] for link in FAR_LINKS], axis=0)
    return with_parts(far.astype(F32) * coef_ref[...])


def inner_walk(scale, band_ref, field_ref, prev_refs, part_ref):
    rows = field_ref.shape[0]
    count = rows // BLK
    for b in range(count):
        block = pl.ds(b * BLK, BLK)
        first, past = max(b - 1, 0), min(b + 2, count)
        value = scale * dot(
            band_ref[block, (first - b + 1) * BLK : (past - b + 1) * BLK],
            field_ref[first * BLK : past * BLK, :],
            ((1,), (0,)),
        )
        for prev_ref in prev_refs:
            value = value - prev_ref[block, :].astype(F32)
        part_ref[block, :] = value


def inside_of(ref):
    return slice(BLK, ref.shape[0] - BLK)


def picked_parts(pick_mat_ref, part_ref):
    inside = inside_of(part_ref)
    both = dot(pick_mat_ref[:, inside], with_parts(part_ref[inside, :]), ((1,), (0,)))
    return parts_joined(both)


def opening_kernel(scale, band_ref, hot_ref, pick_mat_ref, field_ref, part_ref, picked_ref, joint_ref):
    inner_walk(scale, band_ref, field_ref, (), part_ref)
    picked_ref[...] = picked_parts(pick_mat_ref, part_ref)
    inside = inside_of(hot_ref)
    joint = dot(pick_mat_ref[:, inside], hot_ref[inside, :], ((1,), (0,)))
    joint_ref[...] = joint.astype(BF16)


def opening(scale, band, hot, pick_mat, field):
    rows, edges = hot.shape
    return pl.pallas_call(
        lambda *refs: opening_kernel(scale, *refs),
        out_shape=(
            jax.ShapeDtypeStruct((rows, VECS), F32),
            jax.ShapeDtypeStruct((edges, VECS), F32),
            jax.ShapeDtypeStruct((edges, edges), BF16),
        ),
        in_specs=[VMEM] * 4,
        out_specs=(VMEM,) * 3,
        compiler_params=PARAMS,
        cost_estimate=estimate(rows),
        name="opening",
    )(band, hot, pick_mat, field)


def estimate(rows):
    return pl.CostEstimate(
        flops=2 * rows * 3 * BLK * VECS, bytes_accessed=4 * rows * 3 * BLK, transcendentals=0
    )


def inner_kernel(scale, before_scale, more, *refs):
    band_ref, hot_ref, pick_mat_ref, known_ref, far_ref, edge_ref, prev_ref = refs[:7]
    part_ref, more_refs, packed_ref = refs[7], refs[8:-1], refs[-1]
    rows = known_ref.shape[0]
    count = rows // BLK
    for b in range(count):
        block = pl.ds(b * BLK, BLK)
        if b == 0:
            value = edge_ref[:BLK, :]
        elif b == count - 1:
            value = edge_ref[BLK:, :]
        else:
            both = dot(hot_ref[block, :], far_ref[...], ((1,), (0,)))
            value = known_ref[block, :] + parts_joined(both) * before_scale
        if more:
            more_refs[0][block, :] = value
        packed_ref[block, :] = value.astype(BF16)
    inner_walk(scale, band_ref, packed_ref, (prev_ref,), part_ref)
    if more:
        more_refs[1][...] = picked_parts(pick_mat_ref, part_ref)


def inner(scale, before_scale, more, band, hot, pick_mat, known, far, edge, prev):
    rows, edges = hot.shape
    return pl.pallas_call(
        lambda *refs: inner_kernel(scale, before_scale, more, *refs),
        out_shape=(
            jax.ShapeDtypeStruct((rows, VECS), F32),
            *(
                jax.ShapeDtypeStruct((rows, VECS), F32),
                jax.ShapeDtypeStruct((edges, VECS), F32),
            )[: 2 * more],
        ),
        in_specs=[VMEM] * 7,
        out_specs=(VMEM,) * (1 + 2 * more),
        scratch_shapes=[pltpu.VMEM((rows, VECS), BF16)],
        compiler_params=PARAMS,
        cost_estimate=estimate(rows),
        name="inner",
    )(band, hot, pick_mat, known, far, edge, prev)


def advance(place_ref, band_ref, hot_ref, coef_ref, part_ref, got, scale, store, blocks):
    rows = part_ref.shape[0]
    count = rows // BLK
    even = is_low(place_ref, 1)
    got = dict(zip(LINKS, got, strict=True))
    low = jnp.where(even, got[1, 1][...], got[1, 0][...])
    high = jnp.where(even, got[1, 0][...], got[1, 1][...])
    far = far_parts(coef_ref, got)
    for b in blocks:
        block = pl.ds(b * BLK, BLK)
        total = parts_joined(dot(hot_ref[block, :], far, ((1,), (0,))))
        if b == 0:
            total += dot(band_ref[block, :BLK], low, ((1,), (0,)))
        if b == count - 1:
            total += dot(band_ref[block, 2 * BLK :], high, ((1,), (0,)))
        store(block, part_ref[block, :] + total * scale)
    return even, far


def step_kernel(scale, *refs):
    place_ref, band_ref, hot_ref, coef_ref, joint_ref, pick_mat_ref, part_ref, picked_ref = refs[:8]
    got, sent, (far_ref, edge_ref) = refs[8:14], refs[14:20], refs[20:]
    rows = part_ref.shape[0]
    ends = []

    def store(block, value):
        edge_ref[pl.ds(len(ends) * BLK, BLK), :] = value
        ends.append(value.astype(BF16))

    even, far = advance(
        place_ref,
        band_ref,
        hot_ref,
        coef_ref,
        part_ref,
        got,
        scale,
        store,
        (0, rows // BLK - 1),
    )
    far_ref[...] = far
    first, last = ends
    picked = picked_ref[...] + parts_joined(dot(joint_ref[...], far, ((1,), (0,)))) * scale
    picked += dot(pick_mat_ref[:, :BLK], first, ((1,), (0,)))
    picked += dot(pick_mat_ref[:, rows - BLK :], last, ((1,), (0,)))
    send_out(even, first, last, picked, sent)


def step(scale, place, mats, part, picked, got):
    edges = picked.shape[0]
    *sent, far, edge = pl.pallas_call(
        lambda *refs: step_kernel(scale, *refs),
        out_shape=(
            *SENT,
            jax.ShapeDtypeStruct((edges, 2 * VECS), BF16),
            jax.ShapeDtypeStruct((2 * BLK, VECS), F32),
        ),
        in_specs=[SMEM] + [VMEM] * 13,
        out_specs=(VMEM,) * 8,
        compiler_params=PARAMS,
        name="step",
    )(place, *mats, part, picked, *got)
    return sent, far, edge


def last_kernel(scale, *refs):
    place_ref, band_ref, hot_ref, coef_ref, part_ref = refs[:5]
    got, (next_ref, kept_ref, sent_ref) = refs[5:11], refs[11:]

    def store(block, value):
        next_ref[block, :] = with_parts(value)

    advance(
        place_ref,
        band_ref,
        hot_ref,
        coef_ref,
        part_ref,
        got,
        scale,
        store,
        range(part_ref.shape[0] // BLK),
    )
    value = next_ref[...]
    gram = parts_joined(dot(value, value, ((0,), (0,))))
    gram = gram[:VECS] + gram[VECS:]
    half = VECS // 2
    low = is_low(place_ref, 1)
    kept_ref[...] = jnp.where(low, gram[:half], gram[half:])
    sent_ref[...] = jnp.where(low, gram[half:], gram[:half])


def last(scale, place, mats, part, got):
    rows = part.shape[0]
    return pl.pallas_call(
        lambda *refs: last_kernel(scale, *refs),
        out_shape=(
            jax.ShapeDtypeStruct((rows, 2 * VECS), BF16),
            *(jax.ShapeDtypeStruct((VECS // 2, VECS), F32),) * 2,
        ),
        in_specs=[SMEM] + [VMEM] * 10,
        out_specs=(VMEM,) * 3,
        compiler_params=PARAMS,
        name="last",
    )(place, *mats, part, *got)


def total_of(terms):
    terms = list(terms)
    while len(terms) > 1:
        pairs = [terms[i] + terms[i + 1] for i in range(0, len(terms) - 1, 2)]
        terms = pairs + terms[len(terms) - len(terms) % 2 :]
    return terms[0]


def finish_kernel(scale, place_ref, own_ref, other_ref, field_ref, out_ref, inverse_ref):
    width = 8
    shape = (width, VECS)
    panels = VECS // width
    ids = lax.broadcasted_iota(jnp.int32, shape, 0)
    lanes = lax.broadcasted_iota(jnp.int32, shape, 1)

    def spread(value):
        return jnp.broadcast_to(value, shape)

    low = is_low(place_ref, 1)
    gram = jnp.concatenate(
        [
            jnp.where(low, own_ref[...], other_ref[...]),
            jnp.where(low, other_ref[...], own_ref[...]),
        ],
        axis=0,
    )
    left = [gram[width * b : width * (b + 1), :] for b in range(panels)]
    right = [jnp.where(ids + width * b == lanes, 1.0, 0.0) for b in range(panels)]
    for p in range(panels):
        base = width * p
        columns = [spread(left[p][:, base + c : base + c + 1]) for c in range(width)]
        entry = {
            (i, c): spread(columns[c][i : i + 1, :]) for i in range(width) for c in range(i + 1)
        }
        inverse, l, n = [], {}, {}
        for j in range(width):
            inverse.append(1.0 / entry[j, j])
            for i in range(j + 1, width):
                l[i, j] = entry[i, j] * inverse[j]
            for c in range(j + 1, width):
                for i in range(c, width):
                    entry[i, c] = entry[i, c] - l[i, j] * entry[c, j]
        for j in range(width):
            for i in range(j + 1, width):
                n[i, j] = -total_of([l[i, j], *(l[i, m] * n[m, j] for m in range(j + 1, i))])
        factors = []
        for side in (left, right):
            raw = [spread(side[p][i : i + 1, :]) for i in range(width)]
            done = [total_of([raw[i], *(n[i, j] * raw[j] for j in range(i))]) for i in range(width)]
            if side is right:
                for i in range(width):
                    row = done[i] * (lax.rsqrt(entry[i, i]) * scale)
                    inverse_ref[base + i : base + i + 1, :] = row[:1, :]
            done = [d * v for d, v in zip(done, inverse)]
            factors.append(
                [
                    total_of([done[c], *(n[i, c] * done[i] for i in range(c + 1, width))])
                    for c in range(width)
                ]
            )
        for b in range(p + 1, panels):
            columns = [spread(left[b][:, base + c : base + c + 1]) for c in range(width)]
            for side, rows in zip((left, right), factors):
                side[b] = side[b] - total_of(c * r for c, r in zip(columns, rows))
    factor = inverse_ref[...]
    high = factor.astype(BF16)
    rest = (factor - high.astype(F32)).astype(BF16)
    factor = jnp.concatenate(
        [
            jnp.concatenate([high, high], axis=1),
            jnp.concatenate([rest, jnp.zeros_like(rest)], axis=1),
        ],
        axis=0,
    )
    out_ref[...] = parts_joined(dot(field_ref[...], factor, ((1,), (1,))))


def finish(scale, place, halves, field):
    return pl.pallas_call(
        lambda *refs: finish_kernel(scale, *refs),
        out_shape=jax.ShapeDtypeStruct((field.shape[0], VECS), F32),
        in_specs=[SMEM] + [VMEM] * 3,
        out_specs=VMEM,
        scratch_shapes=[pltpu.VMEM((VECS, VECS), F32)],
        compiler_params=PARAMS,
        name="finish",
    )(place, *halves, field)


def summed(kept, sent, count):
    def swapped(value, mask):
        return lax.ppermute(value, AXES, [(i, i ^ mask) for i in range(count)])

    bits = [1 << i for i in range(1, count.bit_length() - 1)]
    half = kept + swapped(sent, 1)
    for i in range(0, len(bits), 2):
        stage = bits[i : i + 2]
        masks = stage if len(stage) == 1 else [*stage, stage[0] ^ stage[1]]
        half = sum((swapped(half, mask) for mask in masks), half)
    return half, swapped(half, 1)


def local(start_basis, band_cols, band_wts, far_dst, far_src, far_wts):
    count = lax.axis_size(AXES)
    place = lax.axis_index(AXES)
    total_rows = start_basis.shape[0] * count

    def swap(value, by, odd):
        return lax.ppermute(value, AXES, swap_pairs(count, by, odd))

    def as_row(value):
        return value.reshape(1, -1)

    asked = as_row(far_src)
    wanted = [swap(asked, *link) for link in FAR_LINKS]
    here = place.astype(jnp.int32).reshape(1)
    band, hot, coef, field = prepare(
        here,
        *(
            pltpu.with_memory_space_constraint(v, pltpu.HBM)
            for v in (
                as_row(far_dst),
                as_row(far_wts),
                jnp.transpose(band_wts, (1, 2, 0)),
                jnp.transpose(band_cols, (1, 2, 0)),
                start_basis,
            )
        ),
    )
    wanted, band = lax.optimization_barrier((wanted, band))
    pick_mat, *sent = first(here, field, wanted)

    def exchange(sent):
        return [swap(v, *link) for v, link in zip(sent, LINKS, strict=True)]

    got = exchange(sent)
    before, scale = 1.0 / HALF_WIDTH, 2.0 / HALF_WIDTH
    part, picked, joint = opening(before, band, hot, pick_mat, field)
    previous = field
    for k in range(1, DEGREE):
        mats = (band, hot, coef, joint, pick_mat)
        sent, far, edge = step(before, here, mats, part, picked, got)
        got = exchange(sent)
        more = k < DEGREE - 1
        part, *rest = inner(scale, before, more, band, hot, pick_mat, part, far, edge, previous)
        if more:
            previous, picked = rest
        before = scale
    filtered, kept, sent = last(scale, here, (band, hot, coef), part, got)
    return finish(math.sqrt(total_rows), here, summed(kept, sent, count), filtered)


def solution(mesh):
    placed = (
        P(AXES, None),
        P(AXES, None, None),
        P(AXES, None, None),
        P(AXES),
        P(AXES),
        P(AXES),
    )
    return jax.shard_map(
        local, mesh=mesh, in_specs=placed, out_specs=P(AXES, None), check_vma=False
    )
```

```python
import math

import jax
import jax.numpy as jnp
from jax import lax
from jax.experimental import pallas as pl
from jax.experimental.pallas import tpu as pltpu
from jax.sharding import PartitionSpec as P

VECS = 128
BLK = 128
KB = 8
PEERS = 4
CAP = 64
DEGREE = 8
HALF_WIDTH = 0.95
AXES = ("row", "snk")
FAR = (2, 4)
LINKS = ((4, 1), (2, 1), (1, 1), (4, 0), (2, 0), (1, 0))
FAR_LINKS = tuple((by, odd) for by in FAR for odd in (0, 1))
BF16 = jnp.bfloat16
F32 = jnp.float32
VMEM = pl.BlockSpec(memory_space=pltpu.VMEM)
HBM = pl.BlockSpec(memory_space=pltpu.HBM)
SMEM = pl.BlockSpec(memory_space=pltpu.SMEM)
PARAMS = pltpu.CompilerParams(vmem_limit_bytes=24 * 1024 * 1024)


def swap_pairs(count, by, odd):
    pairs = []
    for low in range(count):
        if (low // by) % 2 == odd:
            high = (low + by) % count
            pairs += [(low, high), (high, low)]
    return pairs


def split3(value):
    high = value.astype(BF16)
    rest = value - high.astype(F32)
    mid = rest.astype(BF16)
    low = (rest - mid.astype(F32)).astype(BF16)
    return high, mid, low


def stacked(value, height):
    parts = split3(value)
    pad = jnp.zeros((height - 3, value.shape[1]), BF16)
    return jnp.concatenate([*parts, pad], axis=0)


def dot(a, b, dims, precision=None):
    return lax.dot_general(
        a, b, (dims, ((), ())), precision=precision, preferred_element_type=F32
    )


def is_low(place_ref, by):
    return lax.rem(lax.div(place_ref[0], by), 2) == 0


def turned(row):
    half = row.shape[1] // 2
    return jnp.concatenate([row[:, half:], row[:, :half]], axis=1)


def by_link(place_ref, row):
    parts = []
    for i, by in enumerate(FAR):
        pair = row[:, 2 * CAP * i : 2 * CAP * (i + 1)]
        parts.append(jnp.where(is_low(place_ref, by), pair, turned(pair)))
    return jnp.concatenate(parts, axis=1)


def as_rows(row):
    return jnp.concatenate([jnp.broadcast_to(row, (16, row.shape[1])).astype(BF16)] * (BLK // 16), axis=0)


def as_columns(row):
    return jnp.broadcast_to(row, (row.shape[1], row.shape[1])).T


def prepare_kernel(
    place_ref,
    dst_any,
    far_any,
    wts_any,
    cols_any,
    field_any,
    band_ref,
    hot_ref,
    coef_ref,
    field_ref,
    dst_ref,
    far_ref,
    wts_ref,
    cols_ref,
    sems,
):
    copies = [
        pltpu.make_async_copy(source, target, sems.at[i])
        for i, (source, target) in enumerate(
            (
                (dst_any, dst_ref),
                (far_any, far_ref),
                (wts_any, wts_ref),
                (cols_any, cols_ref),
                (field_any, field_ref),
            )
        )
    ]
    for copy in copies:
        copy.start()
    copies[0].wait()
    copies[1].wait()
    rows = cols_ref.shape[2]
    edges = dst_ref.shape[1]
    dst = by_link(place_ref, dst_ref[...])
    far = by_link(place_ref, far_ref[...])
    one, zero = jnp.ones((), BF16), jnp.zeros((), BF16)
    ids = lax.broadcasted_iota(jnp.int32, (BLK, edges), 0).astype(F32).astype(BF16)
    in_block = jnp.where(ids == as_rows(lax.rem(dst, BLK).astype(F32)), one, zero)
    owner = lax.div(dst, BLK)
    for b in range(rows // BLK):
        hot_ref[pl.ds(b * BLK, BLK), :] = in_block * as_rows(jnp.where(owner == b, 1.0, 0.0))
    hot = hot_ref[...]
    degree = jnp.sum(dot(stacked(far, 16), hot, ((1,), (1,))), axis=0, keepdims=True)
    copies[2].wait()
    for o in range(3):
        degree = degree + jnp.sum(wts_ref[o], axis=0, keepdims=True)
    at_edge = jnp.sum(dot(stacked(degree, 16), hot, ((1,), (0,))), axis=0, keepdims=True)
    far_coef = far / at_edge
    for i in range(edges // BLK):
        coef_ref[pl.ds(i * BLK, BLK), :] = as_columns(far_coef[:, i * BLK : (i + 1) * BLK])
    copies[3].wait()
    ids = ids[:, :BLK]
    for b in range(rows // BLK):
        block = pl.ds(b * BLK, BLK)
        degree_b = degree[:, b * BLK : (b + 1) * BLK]
        for o in range(3):
            cols = cols_ref[o, :, block].astype(F32)
            coef = wts_ref[o, :, block] / degree_b
            dense = jnp.zeros((BLK, BLK), BF16)
            for k in range(KB):
                here = ids == as_rows(cols[k : k + 1, :])
                dense = jnp.where(here, as_rows(coef[k : k + 1, :]), dense)
            band_ref[block, pl.ds(o * BLK, BLK)] = dense.T
    copies[4].wait()


def prepare(place, dst, far, wts, cols, field):
    rows, edges = cols.shape[2], dst.shape[1]
    return pl.pallas_call(
        prepare_kernel,
        out_shape=(
            jax.ShapeDtypeStruct((rows, 3 * BLK), BF16),
            jax.ShapeDtypeStruct((rows, edges), BF16),
            jax.ShapeDtypeStruct((edges, VECS), F32),
            jax.ShapeDtypeStruct(field.shape, BF16),
        ),
        in_specs=[SMEM, *(HBM,) * 5],
        out_specs=(VMEM,) * 4,
        scratch_shapes=[
            pltpu.VMEM(dst.shape, jnp.int32),
            pltpu.VMEM(far.shape, F32),
            pltpu.VMEM(wts.shape, F32),
            pltpu.VMEM(cols.shape, jnp.int32),
            pltpu.SemaphoreType.DMA((5,)),
        ],
        compiler_params=PARAMS,
        name="prepare",
    )(place, dst, far, wts, cols, field)


def send_out(even, first, last, picked, sent):
    sent = dict(zip(LINKS, sent, strict=True))
    sent[1, 0][...] = jnp.where(even, last, first)
    sent[1, 1][...] = jnp.where(even, first, last)
    for g, link in enumerate(FAR_LINKS):
        sent[link][:CAP, :] = picked[g * CAP : (g + 1) * CAP].astype(BF16)


def first_kernel(place_ref, field_ref, w0, w1, w2, w3, pick_mat_ref, *sent):
    rows = field_ref.shape[0]
    half = 2 * CAP
    lanes = lax.broadcasted_iota(jnp.int32, (1, half), 1)
    one, zero = jnp.ones((), BF16), jnp.zeros((), BF16)
    for i, (by, pair) in enumerate(zip(FAR, ((w0, w1), (w2, w3)), strict=True)):
        ahead, back = (w[:, i * half : (i + 1) * half] for w in pair)
        low = is_low(place_ref, by)
        ahead = jnp.where(low, turned(ahead), ahead)
        back = jnp.where(low, turned(back), back)
        wanted = jnp.where(lanes < CAP, ahead, back)
        column = as_columns(lax.rem(wanted, BLK).astype(F32)).astype(BF16)
        owner = as_columns(lax.div(wanted, BLK).astype(F32)).astype(BF16)
        ids = lax.broadcasted_iota(jnp.int32, (half, BLK), 1).astype(F32).astype(BF16)
        in_block = jnp.where(column == ids, one, zero)
        for b in range(rows // BLK):
            hot = jnp.where(owner == jnp.full((), b, BF16), in_block, zero)
            pick_mat_ref[pl.ds(i * half, half), pl.ds(b * BLK, BLK)] = hot
    field = field_ref[...]
    picked = dot(pick_mat_ref[...], field, ((1,), (0,)))
    send_out(is_low(place_ref, 1), field[:BLK], field[rows - BLK :], picked, sent)


SENT = tuple(jax.ShapeDtypeStruct((BLK, VECS), BF16) for _ in LINKS)


def first(place, field, wanted):
    rows = field.shape[0]
    return pl.pallas_call(
        first_kernel,
        out_shape=(jax.ShapeDtypeStruct((PEERS * CAP, rows), BF16), *SENT),
        in_specs=[SMEM] + [VMEM] * 5,
        out_specs=(VMEM,) * 7,
        compiler_params=PARAMS,
        name="first",
    )(place, field, *wanted)


def with_parts(value):
    high = value.astype(BF16)
    low = (value - high.astype(F32)).astype(BF16)
    return jnp.concatenate([high, low], axis=1)


def parts_joined(both):
    half = both.shape[1] // 2
    return both[:, :half] + both[:, half:]


def far_parts(coef_ref, got):
    far = jnp.concatenate([got[link][:CAP, :] for link in FAR_LINKS], axis=0)
    return with_parts(far.astype(F32) * coef_ref[...])


def inner_walk(scale, band_ref, field_ref, prev_refs, part_ref):
    rows = field_ref.shape[0]
    count = rows // BLK
    for b in range(count):
        block = pl.ds(b * BLK, BLK)
        first, past = max(b - 1, 0), min(b + 2, count)
        value = scale * dot(
            band_ref[block, (first - b + 1) * BLK : (past - b + 1) * BLK],
            field_ref[first * BLK : past * BLK, :],
            ((1,), (0,)),
        )
        for prev_ref in prev_refs:
            value = value - prev_ref[block, :].astype(F32)
        part_ref[block, :] = value


def inside_of(ref):
    return slice(BLK, ref.shape[0] - BLK)


def picked_parts(pick_mat_ref, part_ref):
    inside = inside_of(part_ref)
    both = dot(pick_mat_ref[:, inside], with_parts(part_ref[inside, :]), ((1,), (0,)))
    return parts_joined(both)


def opening_kernel(scale, band_ref, hot_ref, pick_mat_ref, field_ref, part_ref, picked_ref, joint_ref):
    inner_walk(scale, band_ref, field_ref, (), part_ref)
    picked_ref[...] = picked_parts(pick_mat_ref, part_ref)
    inside = inside_of(hot_ref)
    joint = dot(pick_mat_ref[:, inside], hot_ref[inside, :], ((1,), (0,)))
    joint_ref[...] = joint.astype(BF16)


def opening(scale, band, hot, pick_mat, field):
    rows, edges = hot.shape
    return pl.pallas_call(
        lambda *refs: opening_kernel(scale, *refs),
        out_shape=(
            jax.ShapeDtypeStruct((rows, VECS), F32),
            jax.ShapeDtypeStruct((edges, VECS), F32),
            jax.ShapeDtypeStruct((edges, edges), BF16),
        ),
        in_specs=[VMEM] * 4,
        out_specs=(VMEM,) * 3,
        compiler_params=PARAMS,
        cost_estimate=estimate(rows),
        name="opening",
    )(band, hot, pick_mat, field)


def estimate(rows):
    return pl.CostEstimate(
        flops=2 * rows * 3 * BLK * VECS, bytes_accessed=4 * rows * 3 * BLK, transcendentals=0
    )


def inner_kernel(scale, before_scale, more, *refs):
    band_ref, hot_ref, pick_mat_ref, known_ref, far_ref, edge_ref, prev_ref = refs[:7]
    part_ref, more_refs, packed_ref = refs[7], refs[8:-1], refs[-1]
    rows = known_ref.shape[0]
    count = rows // BLK
    for b in range(count):
        block = pl.ds(b * BLK, BLK)
        if b == 0:
            value = edge_ref[:BLK, :]
        elif b == count - 1:
            value = edge_ref[BLK:, :]
        else:
            both = dot(hot_ref[block, :], far_ref[...], ((1,), (0,)))
            value = known_ref[block, :] + parts_joined(both) * before_scale
        if more:
            more_refs[0][block, :] = value
        packed_ref[block, :] = value.astype(BF16)
    inner_walk(scale, band_ref, packed_ref, (prev_ref,), part_ref)
    if more:
        more_refs[1][...] = picked_parts(pick_mat_ref, part_ref)


def inner(scale, before_scale, more, band, hot, pick_mat, known, far, edge, prev):
    rows, edges = hot.shape
    return pl.pallas_call(
        lambda *refs: inner_kernel(scale, before_scale, more, *refs),
        out_shape=(
            jax.ShapeDtypeStruct((rows, VECS), F32),
            *(
                jax.ShapeDtypeStruct((rows, VECS), F32),
                jax.ShapeDtypeStruct((edges, VECS), F32),
            )[: 2 * more],
        ),
        in_specs=[VMEM] * 7,
        out_specs=(VMEM,) * (1 + 2 * more),
        scratch_shapes=[pltpu.VMEM((rows, VECS), BF16)],
        compiler_params=PARAMS,
        cost_estimate=estimate(rows),
        name="inner",
    )(band, hot, pick_mat, known, far, edge, prev)


def advance(place_ref, band_ref, hot_ref, coef_ref, part_ref, got, scale, store, blocks):
    rows = part_ref.shape[0]
    count = rows // BLK
    even = is_low(place_ref, 1)
    got = dict(zip(LINKS, got, strict=True))
    low = jnp.where(even, got[1, 1][...], got[1, 0][...])
    high = jnp.where(even, got[1, 0][...], got[1, 1][...])
    far = far_parts(coef_ref, got)
    for b in blocks:
        block = pl.ds(b * BLK, BLK)
        total = parts_joined(dot(hot_ref[block, :], far, ((1,), (0,))))
        if b == 0:
            total += dot(band_ref[block, :BLK], low, ((1,), (0,)))
        if b == count - 1:
            total += dot(band_ref[block, 2 * BLK :], high, ((1,), (0,)))
        store(block, part_ref[block, :] + total * scale)
    return even, far


def step_kernel(scale, *refs):
    place_ref, band_ref, hot_ref, coef_ref, joint_ref, pick_mat_ref, part_ref, picked_ref = refs[:8]
    got, sent, (far_ref, edge_ref) = refs[8:14], refs[14:20], refs[20:]
    rows = part_ref.shape[0]
    ends = []

    def store(block, value):
        edge_ref[pl.ds(len(ends) * BLK, BLK), :] = value
        ends.append(value.astype(BF16))

    even, far = advance(
        place_ref,
        band_ref,
        hot_ref,
        coef_ref,
        part_ref,
        got,
        scale,
        store,
        (0, rows // BLK - 1),
    )
    far_ref[...] = far
    first, last = ends
    picked = picked_ref[...] + parts_joined(dot(joint_ref[...], far, ((1,), (0,)))) * scale
    picked += dot(pick_mat_ref[:, :BLK], first, ((1,), (0,)))
    picked += dot(pick_mat_ref[:, rows - BLK :], last, ((1,), (0,)))
    send_out(even, first, last, picked, sent)


def step(scale, place, mats, part, picked, got):
    edges = picked.shape[0]
    *sent, far, edge = pl.pallas_call(
        lambda *refs: step_kernel(scale, *refs),
        out_shape=(
            *SENT,
            jax.ShapeDtypeStruct((edges, 2 * VECS), BF16),
            jax.ShapeDtypeStruct((2 * BLK, VECS), F32),
        ),
        in_specs=[SMEM] + [VMEM] * 13,
        out_specs=(VMEM,) * 8,
        compiler_params=PARAMS,
        name="step",
    )(place, *mats, part, picked, *got)
    return sent, far, edge


def last_kernel(scale, *refs):
    place_ref, band_ref, hot_ref, coef_ref, part_ref = refs[:5]
    got, (next_ref, kept_ref, sent_ref) = refs[5:11], refs[11:]

    def store(block, value):
        next_ref[block, :] = with_parts(value)

    advance(
        place_ref,
        band_ref,
        hot_ref,
        coef_ref,
        part_ref,
        got,
        scale,
        store,
        range(part_ref.shape[0] // BLK),
    )
    value = next_ref[...]
    gram = parts_joined(dot(value, value, ((0,), (0,))))
    gram = gram[:VECS] + gram[VECS:]
    half = VECS // 2
    low = is_low(place_ref, 1)
    kept_ref[...] = jnp.where(low, gram[:half], gram[half:])
    sent_ref[...] = jnp.where(low, gram[half:], gram[:half])


def last(scale, place, mats, part, got):
    rows = part.shape[0]
    return pl.pallas_call(
        lambda *refs: last_kernel(scale, *refs),
        out_shape=(
            jax.ShapeDtypeStruct((rows, 2 * VECS), BF16),
            *(jax.ShapeDtypeStruct((VECS // 2, VECS), F32),) * 2,
        ),
        in_specs=[SMEM] + [VMEM] * 10,
        out_specs=(VMEM,) * 3,
        compiler_params=PARAMS,
        name="last",
    )(place, *mats, part, *got)


def total_of(terms):
    terms = list(terms)
    while len(terms) > 1:
        pairs = [terms[i] + terms[i + 1] for i in range(0, len(terms) - 1, 2)]
        terms = pairs + terms[len(terms) - len(terms) % 2 :]
    return terms[0]


def finish_kernel(scale, place_ref, own_ref, other_ref, field_ref, out_ref, inverse_ref, stage_ref, sems):
    width = 8
    shape = (width, VECS)
    panels = VECS // width
    ids = lax.broadcasted_iota(jnp.int32, shape, 0)
    lanes = lax.broadcasted_iota(jnp.int32, shape, 1)

    def spread(value):
        return jnp.broadcast_to(value, shape)

    low = is_low(place_ref, 1)
    gram = jnp.concatenate(
        [
            jnp.where(low, own_ref[...], other_ref[...]),
            jnp.where(low, other_ref[...], own_ref[...]),
        ],
        axis=0,
    )
    left = [gram[width * b : width * (b + 1), :] for b in range(panels)]
    right = [jnp.where(ids + width * b == lanes, 1.0, 0.0) for b in range(panels)]
    for p in range(panels):
        base = width * p
        columns = [spread(left[p][:, base + c : base + c + 1]) for c in range(width)]
        entry = {
            (i, c): spread(columns[c][i : i + 1, :]) for i in range(width) for c in range(i + 1)
        }
        inverse, l, n = [], {}, {}
        for j in range(width):
            inverse.append(1.0 / entry[j, j])
            for i in range(j + 1, width):
                l[i, j] = entry[i, j] * inverse[j]
            for c in range(j + 1, width):
                for i in range(c, width):
                    entry[i, c] = entry[i, c] - l[i, j] * entry[c, j]
        for j in range(width):
            for i in range(j + 1, width):
                n[i, j] = -total_of([l[i, j], *(l[i, m] * n[m, j] for m in range(j + 1, i))])
        factors = []
        for side in (left, right):
            raw = [spread(side[p][i : i + 1, :]) for i in range(width)]
            done = [total_of([raw[i], *(n[i, j] * raw[j] for j in range(i))]) for i in range(width)]
            if side is right:
                for i in range(width):
                    row = done[i] * (lax.rsqrt(entry[i, i]) * scale)
                    inverse_ref[base + i : base + i + 1, :] = row[:1, :]
            done = [d * v for d, v in zip(done, inverse)]
            factors.append(
                [
                    total_of([done[c], *(n[i, c] * done[i] for i in range(c + 1, width))])
                    for c in range(width)
                ]
            )
        for b in range(p + 1, panels):
            columns = [spread(left[b][:, base + c : base + c + 1]) for c in range(width)]
            for side, rows in zip((left, right), factors):
                side[b] = side[b] - total_of(c * r for c, r in zip(columns, rows))
    factor = inverse_ref[...]
    high = factor.astype(BF16)
    rest = (factor - high.astype(F32)).astype(BF16)
    factor = jnp.concatenate(
        [
            jnp.concatenate([high, high], axis=1),
            jnp.concatenate([rest, jnp.zeros_like(rest)], axis=1),
        ],
        axis=0,
    )
    pieces = sems.shape[0]
    rows = field_ref.shape[0] // pieces
    copies = []
    for i in range(pieces):
        piece = pl.ds(i * rows, rows)
        stage_ref[piece, :] = parts_joined(dot(field_ref[piece, :], factor, ((1,), (1,))))
        copies.append(pltpu.make_async_copy(stage_ref.at[piece], out_ref.at[piece], sems.at[i]))
        copies[i].start()
    for copy in copies:
        copy.wait()


def finish(scale, place, halves, field):
    return pl.pallas_call(
        lambda *refs: finish_kernel(scale, *refs),
        out_shape=jax.ShapeDtypeStruct((field.shape[0], VECS), F32),
        in_specs=[SMEM] + [VMEM] * 3,
        out_specs=HBM,
        scratch_shapes=[
            pltpu.VMEM((VECS, VECS), F32),
            pltpu.VMEM((field.shape[0], VECS), F32),
            pltpu.SemaphoreType.DMA((4,)),
        ],
        compiler_params=PARAMS,
        name="finish",
    )(place, *halves, field)


def summed(kept, sent, count):
    def swapped(value, mask):
        return lax.ppermute(value, AXES, [(i, i ^ mask) for i in range(count)])

    bits = [1 << i for i in range(1, count.bit_length() - 1)]
    half = kept + swapped(sent, 1)
    for i in range(0, len(bits), 2):
        stage = bits[i : i + 2]
        masks = stage if len(stage) == 1 else [*stage, stage[0] ^ stage[1]]
        half = sum((swapped(half, mask) for mask in masks), half)
    return half, swapped(half, 1)


def local(start_basis, band_cols, band_wts, far_dst, far_src, far_wts):
    count = lax.axis_size(AXES)
    place = lax.axis_index(AXES)
    total_rows = start_basis.shape[0] * count

    def swap(value, by, odd):
        return lax.ppermute(value, AXES, swap_pairs(count, by, odd))

    def as_row(value):
        return value.reshape(1, -1)

    asked = as_row(far_src)
    wanted = [swap(asked, *link) for link in FAR_LINKS]
    here = place.astype(jnp.int32).reshape(1)
    band, hot, coef, field = prepare(
        here,
        *(
            pltpu.with_memory_space_constraint(v, pltpu.HBM)
            for v in (
                as_row(far_dst),
                as_row(far_wts),
                jnp.transpose(band_wts, (1, 2, 0)),
                jnp.transpose(band_cols, (1, 2, 0)),
                start_basis,
            )
        ),
    )
    order = (3, 1, 2, 0)
    *turned_round, band = lax.optimization_barrier((*(wanted[i] for i in order), band))
    wanted = [turned_round[order.index(i)] for i in range(PEERS)]
    pick_mat, *sent = first(here, field, wanted)

    def exchange(sent):
        return [swap(v, *link) for v, link in zip(sent, LINKS, strict=True)]

    got = exchange(sent)
    before, scale = 1.0 / HALF_WIDTH, 2.0 / HALF_WIDTH
    part, picked, joint = opening(before, band, hot, pick_mat, field)
    previous = field
    for k in range(1, DEGREE):
        mats = (band, hot, coef, joint, pick_mat)
        sent, far, edge = step(before, here, mats, part, picked, got)
        got = exchange(sent)
        more = k < DEGREE - 1
        part, *rest = inner(scale, before, more, band, hot, pick_mat, part, far, edge, previous)
        if more:
            previous, picked = rest
        before = scale
    filtered, kept, sent = last(scale, here, (band, hot, coef), part, got)
    return finish(math.sqrt(total_rows), here, summed(kept, sent, count), filtered)


def solution(mesh):
    placed = (
        P(AXES, None),
        P(AXES, None, None),
        P(AXES, None, None),
        P(AXES),
        P(AXES),
        P(AXES),
    )
    return jax.shard_map(
        local, mesh=mesh, in_specs=placed, out_specs=P(AXES, None), check_vma=False
    )
```

```python
import math

import jax
import jax.numpy as jnp
from jax import lax
from jax.experimental import pallas as pl
from jax.experimental.pallas import tpu as pltpu
from jax.sharding import PartitionSpec as P

VECS = 128
BLK = 128
KB = 8
PEERS = 4
CAP = 64
DEGREE = 8
HALF_WIDTH = 0.95
AXES = ("row", "snk")
FAR = (2, 4)
LINKS = ((4, 1), (2, 1), (1, 1), (4, 0), (2, 0), (1, 0))
FAR_LINKS = tuple((by, odd) for by in FAR for odd in (0, 1))
BF16 = jnp.bfloat16
F32 = jnp.float32
VMEM = pl.BlockSpec(memory_space=pltpu.VMEM)
HBM = pl.BlockSpec(memory_space=pltpu.HBM)
SMEM = pl.BlockSpec(memory_space=pltpu.SMEM)
PARAMS = pltpu.CompilerParams(vmem_limit_bytes=24 * 1024 * 1024)


def swap_pairs(count, by, odd):
    pairs = []
    for low in range(count):
        if (low // by) % 2 == odd:
            high = (low + by) % count
            pairs += [(low, high), (high, low)]
    return pairs


def split3(value):
    high = value.astype(BF16)
    rest = value - high.astype(F32)
    mid = rest.astype(BF16)
    low = (rest - mid.astype(F32)).astype(BF16)
    return high, mid, low


def stacked(value, height):
    parts = split3(value)
    pad = jnp.zeros((height - 3, value.shape[1]), BF16)
    return jnp.concatenate([*parts, pad], axis=0)


def dot(a, b, dims, precision=None):
    return lax.dot_general(
        a, b, (dims, ((), ())), precision=precision, preferred_element_type=F32
    )


def is_low(place_ref, by):
    return lax.rem(lax.div(place_ref[0], by), 2) == 0


def turned(row):
    half = row.shape[1] // 2
    return jnp.concatenate([row[:, half:], row[:, :half]], axis=1)


def by_link(place_ref, row):
    parts = []
    for i, by in enumerate(FAR):
        pair = row[:, 2 * CAP * i : 2 * CAP * (i + 1)]
        parts.append(jnp.where(is_low(place_ref, by), pair, turned(pair)))
    return jnp.concatenate(parts, axis=1)


def as_rows(row):
    return jnp.concatenate([jnp.broadcast_to(row, (16, row.shape[1])).astype(BF16)] * (BLK // 16), axis=0)


def as_columns(row):
    return jnp.broadcast_to(row, (row.shape[1], row.shape[1])).T


def prepare_kernel(
    place_ref,
    dst_any,
    far_any,
    wts_any,
    cols_any,
    field_any,
    band_ref,
    hot_ref,
    coef_ref,
    field_ref,
    dst_ref,
    far_ref,
    wts_ref,
    cols_ref,
    sems,
):
    copies = [
        pltpu.make_async_copy(source, target, sems.at[i])
        for i, (source, target) in enumerate(
            (
                (dst_any, dst_ref),
                (far_any, far_ref),
                (wts_any, wts_ref),
                (cols_any, cols_ref),
                (field_any, field_ref),
            )
        )
    ]
    for copy in copies:
        copy.start()
    copies[0].wait()
    copies[1].wait()
    rows = cols_ref.shape[2]
    edges = dst_ref.shape[1]
    dst = by_link(place_ref, dst_ref[...])
    far = by_link(place_ref, far_ref[...])
    one, zero = jnp.ones((), BF16), jnp.zeros((), BF16)
    ids = lax.broadcasted_iota(jnp.int32, (BLK, edges), 0).astype(F32).astype(BF16)
    in_block = jnp.where(ids == as_rows(lax.rem(dst, BLK).astype(F32)), one, zero)
    owner = lax.div(dst, BLK)
    for b in range(rows // BLK):
        hot_ref[pl.ds(b * BLK, BLK), :] = in_block * as_rows(jnp.where(owner == b, 1.0, 0.0))
    hot = hot_ref[...]
    degree = jnp.sum(dot(stacked(far, 16), hot, ((1,), (1,))), axis=0, keepdims=True)
    copies[2].wait()
    for o in range(3):
        degree = degree + jnp.sum(wts_ref[o], axis=0, keepdims=True)
    at_edge = jnp.sum(dot(stacked(degree, 16), hot, ((1,), (0,))), axis=0, keepdims=True)
    far_coef = far / at_edge
    for i in range(edges // BLK):
        coef_ref[pl.ds(i * BLK, BLK), :] = as_columns(far_coef[:, i * BLK : (i + 1) * BLK])
    copies[3].wait()
    ids = ids[:, :BLK]
    for b in range(rows // BLK):
        block = pl.ds(b * BLK, BLK)
        degree_b = degree[:, b * BLK : (b + 1) * BLK]
        for o in range(3):
            cols = cols_ref[o, :, block].astype(F32)
            coef = wts_ref[o, :, block] / degree_b
            dense = jnp.zeros((BLK, BLK), BF16)
            for k in range(KB):
                here = ids == as_rows(cols[k : k + 1, :])
                dense = jnp.where(here, as_rows(coef[k : k + 1, :]), dense)
            band_ref[block, pl.ds(o * BLK, BLK)] = dense.T
    copies[4].wait()


def prepare(place, dst, far, wts, cols, field):
    rows, edges = cols.shape[2], dst.shape[1]
    return pl.pallas_call(
        prepare_kernel,
        out_shape=(
            jax.ShapeDtypeStruct((rows, 3 * BLK), BF16),
            jax.ShapeDtypeStruct((rows, edges), BF16),
            jax.ShapeDtypeStruct((edges, VECS), F32),
            jax.ShapeDtypeStruct(field.shape, BF16),
        ),
        in_specs=[SMEM, *(HBM,) * 5],
        out_specs=(VMEM,) * 4,
        scratch_shapes=[
            pltpu.VMEM(dst.shape, jnp.int32),
            pltpu.VMEM(far.shape, F32),
            pltpu.VMEM(wts.shape, F32),
            pltpu.VMEM(cols.shape, jnp.int32),
            pltpu.SemaphoreType.DMA((5,)),
        ],
        compiler_params=PARAMS,
        name="prepare",
    )(place, dst, far, wts, cols, field)


def send_out(even, first, last, picked, sent):
    sent = dict(zip(LINKS, sent, strict=True))
    sent[1, 0][...] = jnp.where(even, last, first)
    sent[1, 1][...] = jnp.where(even, first, last)
    for g, link in enumerate(FAR_LINKS):
        sent[link][:CAP, :] = picked[g * CAP : (g + 1) * CAP].astype(BF16)


def first_kernel(place_ref, field_ref, w0, w1, w2, w3, pick_mat_ref, *sent):
    rows = field_ref.shape[0]
    half = 2 * CAP
    lanes = lax.broadcasted_iota(jnp.int32, (1, half), 1)
    one, zero = jnp.ones((), BF16), jnp.zeros((), BF16)
    for i, (by, pair) in enumerate(zip(FAR, ((w0, w1), (w2, w3)), strict=True)):
        ahead, back = (w[:, i * half : (i + 1) * half] for w in pair)
        low = is_low(place_ref, by)
        ahead = jnp.where(low, turned(ahead), ahead)
        back = jnp.where(low, turned(back), back)
        wanted = jnp.where(lanes < CAP, ahead, back)
        column = as_columns(lax.rem(wanted, BLK).astype(F32)).astype(BF16)
        owner = as_columns(lax.div(wanted, BLK).astype(F32)).astype(BF16)
        ids = lax.broadcasted_iota(jnp.int32, (half, BLK), 1).astype(F32).astype(BF16)
        in_block = jnp.where(column == ids, one, zero)
        for b in range(rows // BLK):
            hot = jnp.where(owner == jnp.full((), b, BF16), in_block, zero)
            pick_mat_ref[pl.ds(i * half, half), pl.ds(b * BLK, BLK)] = hot
    field = field_ref[...]
    picked = dot(pick_mat_ref[...], field, ((1,), (0,)))
    send_out(is_low(place_ref, 1), field[:BLK], field[rows - BLK :], picked, sent)


SENT = tuple(jax.ShapeDtypeStruct((BLK, VECS), BF16) for _ in LINKS)


def first(place, field, wanted):
    rows = field.shape[0]
    return pl.pallas_call(
        first_kernel,
        out_shape=(jax.ShapeDtypeStruct((PEERS * CAP, rows), BF16), *SENT),
        in_specs=[SMEM] + [VMEM] * 5,
        out_specs=(VMEM,) * 7,
        compiler_params=PARAMS,
        name="first",
    )(place, field, *wanted)


def with_parts(value):
    high = value.astype(BF16)
    low = (value - high.astype(F32)).astype(BF16)
    return jnp.concatenate([high, low], axis=1)


def parts_joined(both):
    half = both.shape[1] // 2
    return both[:, :half] + both[:, half:]


def far_parts(coef_ref, got):
    far = jnp.concatenate([got[link][:CAP, :] for link in FAR_LINKS], axis=0)
    return with_parts(far.astype(F32) * coef_ref[...])


def inner_walk(scale, band_ref, field_ref, prev_refs, part_ref):
    rows = field_ref.shape[0]
    count = rows // BLK
    for b in range(count):
        block = pl.ds(b * BLK, BLK)
        first, past = max(b - 1, 0), min(b + 2, count)
        value = scale * dot(
            band_ref[block, (first - b + 1) * BLK : (past - b + 1) * BLK],
            field_ref[first * BLK : past * BLK, :],
            ((1,), (0,)),
        )
        for prev_ref in prev_refs:
            value = value - prev_ref[block, :].astype(F32)
        part_ref[block, :] = value


def inside_of(ref):
    return slice(BLK, ref.shape[0] - BLK)


def picked_parts(pick_mat_ref, part_ref):
    inside = inside_of(part_ref)
    both = dot(pick_mat_ref[:, inside], with_parts(part_ref[inside, :]), ((1,), (0,)))
    return parts_joined(both)


def opening_kernel(scale, band_ref, hot_ref, pick_mat_ref, field_ref, part_ref, picked_ref, joint_ref):
    inner_walk(scale, band_ref, field_ref, (), part_ref)
    picked_ref[...] = picked_parts(pick_mat_ref, part_ref)
    inside = inside_of(hot_ref)
    joint = dot(pick_mat_ref[:, inside], hot_ref[inside, :], ((1,), (0,)))
    joint_ref[...] = joint.astype(BF16)


def opening(scale, band, hot, pick_mat, field):
    rows, edges = hot.shape
    return pl.pallas_call(
        lambda *refs: opening_kernel(scale, *refs),
        out_shape=(
            jax.ShapeDtypeStruct((rows, VECS), F32),
            jax.ShapeDtypeStruct((edges, VECS), F32),
            jax.ShapeDtypeStruct((edges, edges), BF16),
        ),
        in_specs=[VMEM] * 4,
        out_specs=(VMEM,) * 3,
        compiler_params=PARAMS,
        cost_estimate=estimate(rows),
        name="opening",
    )(band, hot, pick_mat, field)


def estimate(rows):
    return pl.CostEstimate(
        flops=2 * rows * 3 * BLK * VECS, bytes_accessed=4 * rows * 3 * BLK, transcendentals=0
    )


def inner_kernel(scale, before_scale, more, *refs):
    band_ref, hot_ref, pick_mat_ref, known_ref, far_ref, edge_ref, prev_ref = refs[:7]
    part_ref, more_refs, packed_ref = refs[7], refs[8:-1], refs[-1]
    rows = known_ref.shape[0]
    count = rows // BLK
    for b in range(count):
        block = pl.ds(b * BLK, BLK)
        if b == 0:
            value = edge_ref[:BLK, :]
        elif b == count - 1:
            value = edge_ref[BLK:, :]
        else:
            both = dot(hot_ref[block, :], far_ref[...], ((1,), (0,)))
            value = known_ref[block, :] + parts_joined(both) * before_scale
        if more:
            more_refs[0][block, :] = value
        packed_ref[block, :] = value.astype(BF16)
    inner_walk(scale, band_ref, packed_ref, (prev_ref,), part_ref)
    if more:
        more_refs[1][...] = picked_parts(pick_mat_ref, part_ref)


def inner(scale, before_scale, more, band, hot, pick_mat, known, far, edge, prev):
    rows, edges = hot.shape
    return pl.pallas_call(
        lambda *refs: inner_kernel(scale, before_scale, more, *refs),
        out_shape=(
            jax.ShapeDtypeStruct((rows, VECS), F32),
            *(
                jax.ShapeDtypeStruct((rows, VECS), F32),
                jax.ShapeDtypeStruct((edges, VECS), F32),
            )[: 2 * more],
        ),
        in_specs=[VMEM] * 7,
        out_specs=(VMEM,) * (1 + 2 * more),
        scratch_shapes=[pltpu.VMEM((rows, VECS), BF16)],
        compiler_params=PARAMS,
        cost_estimate=estimate(rows),
        name="inner",
    )(band, hot, pick_mat, known, far, edge, prev)


def advance(place_ref, band_ref, hot_ref, coef_ref, part_ref, got, scale, store, blocks):
    rows = part_ref.shape[0]
    count = rows // BLK
    even = is_low(place_ref, 1)
    got = dict(zip(LINKS, got, strict=True))
    low = jnp.where(even, got[1, 1][...], got[1, 0][...])
    high = jnp.where(even, got[1, 0][...], got[1, 1][...])
    far = far_parts(coef_ref, got)
    for b in blocks:
        block = pl.ds(b * BLK, BLK)
        total = parts_joined(dot(hot_ref[block, :], far, ((1,), (0,))))
        if b == 0:
            total += dot(band_ref[block, :BLK], low, ((1,), (0,)))
        if b == count - 1:
            total += dot(band_ref[block, 2 * BLK :], high, ((1,), (0,)))
        store(block, part_ref[block, :] + total * scale)
    return even, far


def step_kernel(scale, *refs):
    place_ref, band_ref, hot_ref, coef_ref, joint_ref, pick_mat_ref, part_ref, picked_ref = refs[:8]
    got, sent, (far_ref, edge_ref) = refs[8:14], refs[14:20], refs[20:]
    rows = part_ref.shape[0]
    ends = []

    def store(block, value):
        edge_ref[pl.ds(len(ends) * BLK, BLK), :] = value
        ends.append(value.astype(BF16))

    even, far = advance(
        place_ref,
        band_ref,
        hot_ref,
        coef_ref,
        part_ref,
        got,
        scale,
        store,
        (0, rows // BLK - 1),
    )
    far_ref[...] = far
    first, last = ends
    picked = picked_ref[...] + parts_joined(dot(joint_ref[...], far, ((1,), (0,)))) * scale
    picked += dot(pick_mat_ref[:, :BLK], first, ((1,), (0,)))
    picked += dot(pick_mat_ref[:, rows - BLK :], last, ((1,), (0,)))
    send_out(even, first, last, picked, sent)


def step(scale, place, mats, part, picked, got):
    edges = picked.shape[0]
    *sent, far, edge = pl.pallas_call(
        lambda *refs: step_kernel(scale, *refs),
        out_shape=(
            *SENT,
            jax.ShapeDtypeStruct((edges, 2 * VECS), BF16),
            jax.ShapeDtypeStruct((2 * BLK, VECS), F32),
        ),
        in_specs=[SMEM] + [VMEM] * 13,
        out_specs=(VMEM,) * 8,
        compiler_params=PARAMS,
        name="step",
    )(place, *mats, part, picked, *got)
    return sent, far, edge


def last_kernel(scale, *refs):
    place_ref, band_ref, hot_ref, coef_ref, part_ref = refs[:5]
    got, (next_ref, kept_ref, sent_ref) = refs[5:11], refs[11:]

    def store(block, value):
        next_ref[block, :] = with_parts(value)

    advance(
        place_ref,
        band_ref,
        hot_ref,
        coef_ref,
        part_ref,
        got,
        scale,
        store,
        range(part_ref.shape[0] // BLK),
    )
    value = next_ref[...]
    gram = parts_joined(dot(value, value, ((0,), (0,))))
    gram = gram[:VECS] + gram[VECS:]
    half = VECS // 2
    low = is_low(place_ref, 1)
    kept_ref[...] = jnp.where(low, gram[:half], gram[half:])
    sent_ref[...] = jnp.where(low, gram[half:], gram[:half])


def last(scale, place, mats, part, got):
    rows = part.shape[0]
    return pl.pallas_call(
        lambda *refs: last_kernel(scale, *refs),
        out_shape=(
            jax.ShapeDtypeStruct((rows, 2 * VECS), BF16),
            *(jax.ShapeDtypeStruct((VECS // 2, VECS), F32),) * 2,
        ),
        in_specs=[SMEM] + [VMEM] * 10,
        out_specs=(VMEM,) * 3,
        compiler_params=PARAMS,
        name="last",
    )(place, *mats, part, *got)


def total_of(terms):
    terms = list(terms)
    while len(terms) > 1:
        pairs = [terms[i] + terms[i + 1] for i in range(0, len(terms) - 1, 2)]
        terms = pairs + terms[len(terms) - len(terms) % 2 :]
    return terms[0]


def finish_kernel(scale, place_ref, own_ref, other_ref, field_ref, out_ref, inverse_ref, stage_ref, sems):
    width = 8
    shape = (width, VECS)
    panels = VECS // width
    ids = lax.broadcasted_iota(jnp.int32, shape, 0)
    lanes = lax.broadcasted_iota(jnp.int32, shape, 1)

    def spread(value):
        return jnp.broadcast_to(value, shape)

    low = is_low(place_ref, 1)
    gram = jnp.concatenate(
        [
            jnp.where(low, own_ref[...], other_ref[...]),
            jnp.where(low, other_ref[...], own_ref[...]),
        ],
        axis=0,
    )
    left = [gram[width * b : width * (b + 1), :] for b in range(panels)]
    right = [jnp.where(ids + width * b == lanes, 1.0, 0.0) for b in range(panels)]
    for p in range(panels):
        base = width * p
        columns = [spread(left[p][:, base + c : base + c + 1]) for c in range(width)]
        entry = {
            (i, c): spread(columns[c][i : i + 1, :]) for i in range(width) for c in range(i + 1)
        }
        inverse, l, n = [], {}, {}
        for j in range(width):
            inverse.append(1.0 / entry[j, j])
            for i in range(j + 1, width):
                l[i, j] = entry[i, j] * inverse[j]
            for c in range(j + 1, width):
                for i in range(c, width):
                    entry[i, c] = entry[i, c] - l[i, j] * entry[c, j]
        for j in range(width):
            for i in range(j + 1, width):
                n[i, j] = -total_of([l[i, j], *(l[i, m] * n[m, j] for m in range(j + 1, i))])
        factors = []
        for side in (left, right):
            raw = [spread(side[p][i : i + 1, :]) for i in range(width)]
            done = [total_of([raw[i], *(n[i, j] * raw[j] for j in range(i))]) for i in range(width)]
            if side is right:
                for i in range(width):
                    row = done[i] * (lax.rsqrt(entry[i, i]) * scale)
                    inverse_ref[base + i : base + i + 1, :] = row[:1, :]
            done = [d * v for d, v in zip(done, inverse)]
            factors.append(
                [
                    total_of([done[c], *(n[i, c] * done[i] for i in range(c + 1, width))])
                    for c in range(width)
                ]
            )
        for b in range(p + 1, panels):
            columns = [spread(left[b][:, base + c : base + c + 1]) for c in range(width)]
            for side, rows in zip((left, right), factors):
                side[b] = side[b] - total_of(c * r for c, r in zip(columns, rows))
    factor = inverse_ref[...]
    high = factor.astype(BF16)
    rest = (factor - high.astype(F32)).astype(BF16)
    factor = jnp.concatenate(
        [
            jnp.concatenate([high, high], axis=1),
            jnp.concatenate([rest, jnp.zeros_like(rest)], axis=1),
        ],
        axis=0,
    )
    pieces = sems.shape[0]
    rows = field_ref.shape[0] // pieces
    copies = []
    for i in range(pieces):
        piece = pl.ds(i * rows, rows)
        stage_ref[piece, :] = parts_joined(dot(field_ref[piece, :], factor, ((1,), (1,))))
        copies.append(pltpu.make_async_copy(stage_ref.at[piece], out_ref.at[piece], sems.at[i]))
        copies[i].start()
    for copy in copies:
        copy.wait()


def finish(scale, place, halves, field):
    return pl.pallas_call(
        lambda *refs: finish_kernel(scale, *refs),
        out_shape=jax.ShapeDtypeStruct((field.shape[0], VECS), F32),
        in_specs=[SMEM] + [VMEM] * 3,
        out_specs=HBM,
        scratch_shapes=[
            pltpu.VMEM((VECS, VECS), F32),
            pltpu.VMEM((field.shape[0], VECS), F32),
            pltpu.SemaphoreType.DMA((8,)),
        ],
        compiler_params=PARAMS,
        name="finish",
    )(place, *halves, field)


def summed(kept, sent, count):
    def swapped(value, mask):
        return lax.ppermute(value, AXES, [(i, i ^ mask) for i in range(count)])

    bits = [1 << i for i in range(1, count.bit_length() - 1)]
    half = kept + swapped(sent, 1)
    for i in range(0, len(bits), 2):
        stage = bits[i : i + 2]
        masks = stage if len(stage) == 1 else [*stage, stage[0] ^ stage[1]]
        half = sum((swapped(half, mask) for mask in masks), half)
    return half, swapped(half, 1)


def local(start_basis, band_cols, band_wts, far_dst, far_src, far_wts):
    count = lax.axis_size(AXES)
    place = lax.axis_index(AXES)
    total_rows = start_basis.shape[0] * count

    def swap(value, by, odd):
        return lax.ppermute(value, AXES, swap_pairs(count, by, odd))

    def as_row(value):
        return value.reshape(1, -1)

    asked = as_row(far_src)
    wanted = [swap(asked, *link) for link in FAR_LINKS]
    here = place.astype(jnp.int32).reshape(1)
    band, hot, coef, field = prepare(
        here,
        *(
            pltpu.with_memory_space_constraint(v, pltpu.HBM)
            for v in (
                as_row(far_dst),
                as_row(far_wts),
                jnp.transpose(band_wts, (1, 2, 0)),
                jnp.transpose(band_cols, (1, 2, 0)),
                start_basis,
            )
        ),
    )
    order = (3, 1, 2, 0)
    *turned_round, band = lax.optimization_barrier((*(wanted[i] for i in order), band))
    wanted = [turned_round[order.index(i)] for i in range(PEERS)]
    pick_mat, *sent = first(here, field, wanted)

    def exchange(sent):
        return [swap(v, *link) for v, link in zip(sent, LINKS, strict=True)]

    got = exchange(sent)
    before, scale = 1.0 / HALF_WIDTH, 2.0 / HALF_WIDTH
    part, picked, joint = opening(before, band, hot, pick_mat, field)
    previous = field
    for k in range(1, DEGREE):
        mats = (band, hot, coef, joint, pick_mat)
        sent, far, edge = step(before, here, mats, part, picked, got)
        got = exchange(sent)
        more = k < DEGREE - 1
        part, *rest = inner(scale, before, more, band, hot, pick_mat, part, far, edge, previous)
        if more:
            previous, picked = rest
        before = scale
    filtered, kept, sent = last(scale, here, (band, hot, coef), part, got)
    return finish(math.sqrt(total_rows), here, summed(kept, sent, count), filtered)


def solution(mesh):
    placed = (
        P(AXES, None),
        P(AXES, None, None),
        P(AXES, None, None),
        P(AXES),
        P(AXES),
        P(AXES),
    )
    return jax.shard_map(
        local, mesh=mesh, in_specs=placed, out_specs=P(AXES, None), check_vma=False
    )
```
